128 devices in a mesh: dp: 4 (over x_lo, core), tensor: 32 (over z, y, x_hi).
Axes of the slice: x: 4 (x_hi: 2, x_lo: 2; x = x_hi * 2 + x_lo), y: 4, z: 4, core: 2. Of those that a mesh axis runs over, the one named last changes fastest.
Arguments:
- tokens: bfloat16 [2048, 4096], P(('dp', 'tensor')), may hold values from -6 to 6
- cotangent: bfloat16 [2048, 4096], P(('dp', 'tensor')), may hold values from -6 to 6
- gate_weight: bfloat16 [4096, 14336], P(None, 'tensor'), may hold values from -0.09375 to 0.09375
- up_weight: bfloat16 [4096, 14336], P(None, 'tensor'), may hold values from -0.09375 to 0.09375
- down_weight: bfloat16 [14336, 4096], P('tensor'), may hold values from -0.046875 to 0.046875
Outputs:
- output: bfloat16 [2048, 4096], P(('dp', 'tensor'))
- input_grad: bfloat16 [2048, 4096], P(('dp', 'tensor'))
- gate_grad: bfloat16 [4096, 14336], P('dp', 'tensor')
- up_grad: bfloat16 [4096, 14336], P('dp', 'tensor')
- down_grad: bfloat16 [14336, 4096], P('tensor', 'dp')
The draws below stay inside these ranges and needn't reach their ends.
All inputs are finite; a program needn't handle non-finite values.
Results may differ from the reference program's by a relative error of at most 0.005.
Values may be sent and summed in bfloat16 or wider, within the bound.
A program may use at most 128 MiB of HBM per device.

```python
import jax
import jax.numpy as jnp
from jax import lax

D = 4096
FF = 14336
TOKENS = 2048


def block_scale(own_key, shape, cuts, least, high):
    def one(position, shards_of):
        draws = jax.random.uniform(jax.random.fold_in(jax.random.fold_in(own_key, 6), position), (shards_of,), jnp.float32, least / len(cuts), high / len(cuts))
        return jnp.repeat(jnp.exp(draws), shape[position] // shards_of).reshape((-1,) + (1,) * (len(shape) - position - 1))

    level = one(*cuts[0])
    for cut in cuts[1:]:
        level = level * one(*cut)
    return level


def noise(key, shape, spread, limit, pieces=(), dtype=jnp.bfloat16):
    factor_of = block_scale(key, shape, pieces, -0.22, 0.18) if pieces else 1.0
    array = jax.random.normal(key, shape, jnp.float32) * spread * factor_of
    return jnp.minimum(jnp.maximum(array, -limit), limit).astype(dtype)


def setup_inputs(seed: int = 0) -> dict:
    key_list = jax.random.split(jax.random.key(seed), 6)
    tokens = noise(key_list[0], (TOKENS, D), 1.0, 6.0, ((0, 128),))
    cotangent = noise(key_list[1], (TOKENS, D), 1.0, 6.0, ((0, 128),))
    gate_weight = noise(key_list[2], (D, FF), D ** -0.5, 0.09375, ((1, 32),))
    up_weight = noise(key_list[3], (D, FF), D ** -0.5, 0.09375, ((1, 32),))
    down_weight = noise(key_list[4], (FF, D), FF ** -0.5, 0.046875, ((0, 32),))
    return {"tokens": tokens, "cotangent": cotangent, "gate_weight": gate_weight, "up_weight": up_weight, "down_weight": down_weight}


def contract_rows(left, right):
    return lax.dot_general(left, right, (((0,), (0,)), ((), ())), preferred_element_type=jnp.float32)


def contract_cols(left, right):
    return lax.dot_general(left, right, (((1,), (1,)), ((), ())), preferred_element_type=jnp.float32)


def reference(tokens, cotangent, gate_weight, up_weight, down_weight):
    gate = jnp.dot(tokens, gate_weight, preferred_element_type=jnp.float32)
    up = jnp.dot(tokens, up_weight, preferred_element_type=jnp.float32)
    sig = jax.nn.sigmoid(gate)
    act = gate * sig
    hidden = (act * up).astype(jnp.bfloat16)
    output = jnp.dot(hidden, down_weight, preferred_element_type=jnp.float32).astype(jnp.bfloat16)
    dhidden = contract_cols(cotangent, down_weight)
    dgate = (dhidden * up * sig * (1.0 + gate * (1.0 - sig))).astype(jnp.bfloat16)
    dup = (dhidden * act).astype(jnp.bfloat16)
    input_grad = (contract_cols(dgate, gate_weight) + contract_cols(dup, up_weight)).astype(jnp.bfloat16)
    gate_total = contract_rows(tokens, dgate)
    up_total = contract_rows(tokens, dup)
    down_total = contract_rows(hidden, cotangent)
    return (output, input_grad, gate_total.astype(jnp.bfloat16), up_total.astype(jnp.bfloat16), down_total.astype(jnp.bfloat16))
```

```python
import jax
import jax.numpy as jnp
from jax import lax
from jax.experimental import pallas as pl
from jax.experimental.pallas import tpu as pltpu
from jax.sharding import PartitionSpec as P

MESH = pl.DeviceIdType.MESH
BF16, F32 = jnp.bfloat16, jnp.float32
T, D, H, Q = 512, 4096, 448, 1024


def mm(a, b):
    return jnp.dot(a, b, preferred_element_type=F32)


def mm_nt(a, b):
    return lax.dot_general(a, b, (((1,), (1,)), ((), ())), preferred_element_type=F32)


def kernel(
    tok, cot, wg, wu, wd,
    out, ig, gg, ug, dg,
    X, WG, WU, WD, gate, up, dhid, hid, dgate, dup, hidT, dgT, duT,
    PS, R1, RF, R2, R3, TS, TO, SO, OB, WB, CR, XR,
    ls, gs, gr, ss, sr, cs, cr, xs, xr,
):
    dp, t = lax.axis_index("dp"), lax.axis_index("tensor")
    xl, c = dp // 2, lax.rem(dp, 2)
    z, y, xh = t // 8, lax.rem(t // 2, 4), lax.rem(t, 2)

    def ring(v, off):
        return lax.rem(v + (off + 4) % 4, 4)

    def dev(zz, yy, hh=None):
        return (dp, zz * 8 + yy * 2 + (xh if hh is None else hh))

    x_pair = ((1 - xl) * 2 + c, t)
    core_pair = (xl * 2 + 1 - c, t)
    h_pair = dev(z, y, 1 - xh)
    my_row = pl.multiple_of(xh * 16, 16)
    pair_row = pl.multiple_of((1 - xh) * 16, 16)
    OFFS = (1, -1, 2)

    def at(h, a, b):
        return (b, a) if h == 0 else (a, b)

    me_a, me_b = (y, z), (z, y)

    def peer(h, da=0, db=0):
        return dev(*at(h, ring(me_a[h], da), ring(me_b[h], db)))

    started = []

    def send(src, dst, s, r, to):
        cp = pltpu.make_async_remote_copy(
            src_ref=src, dst_ref=dst, send_sem=s, recv_sem=r, device_id=to, device_id_type=MESH
        )
        cp.start()
        started.append(cp)
        return cp

    def arrived(ref, r):
        pltpu.make_async_copy(ref, ref, r).wait()

    loads = []
    for arr, ref in enumerate((tok, cot)):
        for q in range(4):
            cp = pltpu.make_async_copy(
                ref.at[:, pl.ds(q * Q, Q)], X.at[arr * 4 + q, z, y, pl.ds(my_row, 16)], ls.at[arr * 4 + q]
            )
            cp.start()
            loads.append(cp)
    wloads = [pltpu.make_async_copy(wg, WG, ls.at[8]), pltpu.make_async_copy(wu, WU, ls.at[9])]
    for q in range(4):
        wloads.append(pltpu.make_async_copy(wd.at[:, pl.ds(q * Q, Q)], WD.at[q], ls.at[10 + q]))
    for cp in wloads:
        cp.start()

    barrier = pltpu.get_barrier_semaphore()
    peers = [x_pair, core_pair, h_pair]
    for off in OFFS:
        peers += [dev(ring(z, off), y), dev(z, ring(y, off))]
    for p in peers:
        pl.semaphore_signal(barrier, inc=1, device_id=p, device_id_type=MESH)
    pl.semaphore_wait(barrier, len(peers))

    base = (0, 2, 4 + (1 - xl) * 2, 4 + xl * 2)

    def blk(u, h, a, b):
        return X.at[(base[u] + h,) + at(h, a, b)]

    def sub(u, h, a, b, row):
        return X.at[(base[u] + h,) + at(h, a, b) + (pl.ds(row, 16),)]

    def gsend(u, i, ref, to):
        send(ref, ref, gs.at[u, i], gr.at[u, i], to)

    def g_start(u):
        ref = X.at[pl.ds(base[u], 2), z, y, pl.ds(my_row, 16)]
        gsend(u, 0, ref, h_pair)
        for s, off in enumerate(OFFS):
            for h in range(2):
                gsend(u, 1 + h * 6 + s, sub(u, h, me_a[h], me_b[h], my_row), peer(h, da=off))

    def g_spread(u, s):
        for h in range(2):
            a = me_a[h] if s == 0 else ring(me_a[h], -OFFS[s - 1])
            for d, off in enumerate((1, -1)):
                gsend(u, 13 + h * 8 + s * 2 + d, blk(u, h, a, me_b[h]), peer(h, db=off))

    def g_own(u):
        arrived(X.at[pl.ds(base[u], 2), z, y, pl.ds(pair_row, 16)], gr.at[u, 0])
        for s, off in enumerate(OFFS):
            for h in range(2):
                gsend(u, 4 + h * 6 + s, sub(u, h, me_a[h], me_b[h], pair_row), peer(h, da=off))
        g_spread(u, 0)

    def g_mid(u, s):
        off = OFFS[s - 1]
        for h in range(2):
            a = ring(me_a[h], -off)
            arrived(sub(u, h, a, me_b[h], my_row), gr.at[u, 1 + h * 6 + s - 1])
            arrived(sub(u, h, a, me_b[h], pair_row), gr.at[u, 4 + h * 6 + s - 1])
        g_spread(u, s)

    def g_forward(u, s):
        for h in range(2):
            a = me_a[h] if s == 0 else ring(me_a[h], -OFFS[s - 1])
            for d, off in enumerate((1, -1)):
                b = ring(me_b[h], -off)
                i = h * 8 + s * 2 + d
                arrived(blk(u, h, a, b), gr.at[u, 13 + i])
                gsend(u, 29 + i, sub(u, h, a, b, d * 16), peer(h, db=off))

    def g_done(u):
        for s in range(4):
            for h in range(2):
                a = me_a[h] if s == 0 else ring(me_a[h], -OFFS[s - 1])
                for d in range(2):
                    arrived(sub(u, h, a, ring(me_b[h], 2), d * 16), gr.at[u, 29 + h * 8 + s * 2 + d])

    def rows_of(i, r):
        return X[i, pl.ds(2 * r, 2)].reshape(256, Q)

    def gate_up(w):
        for q in (2 * w, 2 * w + 1):
            def step(r, _):
                x = rows_of(q, r)
                rows = pl.ds(pl.multiple_of(r * 256, 256), 256)
                g = mm(x, WG[pl.ds(q * Q, Q), :])
                u = mm(x, WU[pl.ds(q * Q, Q), :])
                if q == 0:
                    gate[rows, :] = g
                    up[rows, :] = u
                else:
                    gate[rows, :] += g
                    up[rows, :] += u
                return 0

            lax.fori_loop(0, 2, step, 0)

    def hidden():
        def step(r, _):
            rows = pl.ds(pl.multiple_of(r * 32, 32), 32)
            g = gate[rows, :]
            hid[rows, :] = (g * jax.nn.sigmoid(g) * up[rows, :]).astype(BF16)
            return 0

        lax.fori_loop(0, 16, step, 0)

    def backward():
        def step(r, _):
            rows = pl.ds(pl.multiple_of(r * 32, 32), 32)
            g, dh = gate[rows, :], dhid[rows, :]
            sig = jax.nn.sigmoid(g)
            dgate[rows, :] = (dh * up[rows, :] * sig * (1.0 + g * (1.0 - sig))).astype(BF16)
            dup[rows, :] = (dh * (g * sig)).astype(BF16)
            return 0

        lax.fori_loop(0, 16, step, 0)

    def transpose(src, dst):
        for r in range(4):
            dst[:, r * 128:(r + 1) * 128] = src[r * 128:(r + 1) * 128, :].astype(F32).T.astype(BF16)

    def output_part(q):
        def step(r, _):
            rows = pl.ds(pl.multiple_of(r * 256, 256), 256)
            PS[q, pl.ds(2 * r, 2)] = mm(hid[rows, :], WD[q]).astype(BF16).reshape(2, 4, 32, Q)
            return 0

        lax.fori_loop(0, 2, step, 0)

    def dhidden_part(u, first):
        for h in range(2):
            def step(r, _):
                rows = pl.ds(pl.multiple_of(r * 256, 256), 256)
                v = mm_nt(rows_of(base[u] + h, r), WD[base[u] - 4 + h])
                if first and h == 0:
                    dhid[rows, :] = v
                else:
                    dhid[rows, :] += v
                return 0

            lax.fori_loop(0, 2, step, 0)

    def input_part(q):
        def step(r, _):
            rows = pl.ds(pl.multiple_of(r * 256, 256), 256)
            v = mm_nt(dgate[rows, :], WG[pl.ds(q * Q, Q), :]) + mm_nt(dup[rows, :], WU[pl.ds(q * Q, Q), :])
            PS[4 + q, pl.ds(2 * r, 2)] = v.astype(BF16).reshape(2, 4, 32, Q)
            return 0

        lax.fori_loop(0, 2, step, 0)

    def chunk(v, h, b, row, n):
        tail = (pl.ds(row, n), slice(None))
        i = (v // 2) * 4 + (v % 2) * 2 + h
        return (i, b, slice(None)) + tail if h == 0 else (i, slice(None), b) + tail

    def s_first(v):
        for h in range(2):
            for d, off in enumerate((1, -1)):
                k = h * 6 + d * 3
                far, near = ring(me_b[h], 2), ring(me_b[h], off)
                send(PS.at[chunk(v, h, far, d * 16, 16)], RF.at[v, h, d], ss.at[v, k], sr.at[v, k], peer(h, db=off))
                o = (1 - d) * 16
                send(
                    PS.at[chunk(v, h, near, o, 16)], R1.at[v, h, d, :, pl.ds(o, 16)],
                    ss.at[v, k + 1], sr.at[v, k + 1], peer(h, db=off),
                )

    def s_join(v):
        for h in range(2):
            for d, off in enumerate((1, -1)):
                k = h * 6 + d * 3
                near, o = ring(me_b[h], off), d * 16
                arrived(RF.at[v, h, d], sr.at[v, k])
                RF[v, h, d] = (
                    RF[v, h, d].astype(F32) + PS[chunk(v, h, near, o, 16)].astype(F32)
                ).astype(BF16)
                send(
                    RF.at[v, h, d], R1.at[v, h, d, :, pl.ds(o, 16)],
                    ss.at[v, k + 2], sr.at[v, k + 2], peer(h, db=off),
                )

    def s_second(v):
        for h in range(2):
            for d in range(2):
                k = h * 6 + d * 3
                arrived(R1.at[v, h, d, :, pl.ds((1 - d) * 16, 16)], sr.at[v, k + 1])
                arrived(R1.at[v, h, d, :, pl.ds(d * 16, 16)], sr.at[v, k + 2])
            i = (v // 2) * 4 + (v % 2) * 2 + h

            def total(a):
                own = PS[(i,) + at(h, a, me_b[h])].astype(F32)
                return own + R1[v, h, 0, a].astype(F32) + R1[v, h, 1, a].astype(F32)

            for s, off in enumerate(OFFS):
                a = ring(me_a[h], off)
                mine = (i,) + at(h, a, me_b[h])
                PS[mine] = total(a).astype(BF16)
                k = 12 + h * 3 + s
                send(PS.at[mine], R2.at[v, h, s], ss.at[v, k], sr.at[v, k], peer(h, da=off))
            SO[v, h] = total(me_a[h])

    def s_third(v):
        for h in range(2):
            for s in range(3):
                arrived(R2.at[v, h, s], sr.at[v, 12 + h * 3 + s])
            SO[v, h] = (
                SO[v, h] + R2[v, h, 0].astype(F32) + R2[v, h, 1].astype(F32) + R2[v, h, 2].astype(F32)
            )
            TO[v, h] = SO[v, h, pl.ds(my_row, 16)]
            TS[v, h] = SO[v, h, pl.ds(pair_row, 16)].astype(BF16)
        send(TS.at[v], R3.at[v], ss.at[v, 18], sr.at[v, 18], h_pair)

    stores = []

    def s_finish(v):
        arrived(R3.at[v], sr.at[v, 18])
        for h in range(2):
            q = (v % 2) * 2 + h
            OB[v // 2, :, q * Q:(q + 1) * Q] = (TO[v, h] + R3[v, h].astype(F32)).astype(BF16)
        if v % 2 == 1:
            cp = pltpu.make_async_copy(OB.at[v // 2], (out, ig)[v // 2], ls.at[14 + v // 2])
            cp.start()
            stores.append(cp)

    lhs, x0 = (hidT, dgT, duT), (4, 0, 0)
    jobs = {}

    def w_part(j):
        arr, w = j % 3, (1 - xl) if j < 3 else xl
        if j >= 2:
            jobs[j - 2].wait_send()
            started[:] = [cp for cp in started if cp is not jobs[j - 2]]

        def step(k, _):
            quarter = w * 2 + jnp.where(k == 0, 1 - c, c)
            slot = jnp.where(k == 0, 6 + j % 2, j)
            for n in range(2):
                xb = X[x0[arr] + quarter, :, :, :, n * 512:(n + 1) * 512].reshape(T, 512)
                WB[slot, :, n * 512:(n + 1) * 512] = mm(lhs[arr][...], xb).astype(BF16)
            return 0

        lax.fori_loop(0, 2, step, 0)
        jobs[j] = send(WB.at[6 + j % 2], CR.at[j], cs.at[j], cr.at[j], core_pair)

    def w_cross(j):
        arrived(CR.at[j], cr.at[j])

        def step(r, _):
            rows = pl.ds(pl.multiple_of(r * 64, 64), 64)
            WB[j, rows, :] = (WB[j, rows, :].astype(F32) + CR[j, rows, :].astype(F32)).astype(BF16)
            return 0

        lax.fori_loop(0, 7, step, 0)
        send(WB.at[j], XR.at[j], xs.at[j], xr.at[j], x_pair)

    def w_finish(arr):
        j = 3 + arr
        arrived(CR.at[j], cr.at[j])
        arrived(XR.at[arr], xr.at[arr])
        if arr == 0:
            def step(r, _):
                rows = pl.ds(pl.multiple_of(r * 64, 64), 64)
                v = WB[j, rows, :].astype(F32) + CR[j, rows, :].astype(F32) + XR[arr, rows, :].astype(F32)
                WB[j, rows, :] = v.astype(BF16)
                return 0

            lax.fori_loop(0, 7, step, 0)
            cp = pltpu.make_async_copy(WB.at[j], dg, ls.at[16])
        else:
            buf = (WG, WU)[arr - 1]
            for n in range(8):
                cols = slice(n * 128, (n + 1) * 128)
                v = WB[j, :, cols].astype(F32) + CR[j, :, cols].astype(F32) + XR[arr, :, cols].astype(F32)
                buf[cols, :] = v.T.astype(BF16)
            cp = pltpu.make_async_copy(buf.at[pl.ds(0, Q)], (gg, ug)[arr - 1], ls.at[16 + arr])
        cp.start()
        stores.append(cp)

    for cp in loads:
        cp.wait()
    g_start(0)
    g_own(0)
    g_start(1)
    for s in (1, 2, 3):
        g_mid(0, s)
    g_forward(0, 0)
    g_own(1)
    for s in (1, 2, 3):
        g_forward(0, s)
    g_start(2)
    for s in (1, 2, 3):
        g_mid(1, s)
    g_done(0)
    for cp in wloads:
        cp.wait()
    gate_up(0)
    g_own(2)
    for s in range(4):
        g_forward(1, s)
    g_start(3)
    for s in (1, 2, 3):
        g_mid(2, s)
    g_done(1)
    gate_up(1)
    g_own(3)
    for s in range(4):
        g_forward(2, s)
    hidden()
    for s in (1, 2, 3):
        g_mid(3, s)
    transpose(hid, hidT)
    g_done(2)
    w_part(0)
    for s in range(4):
        g_forward(3, s)
    w_cross(0)
    output_part(0)
    output_part(1)
    s_first(0)
    output_part(2)
    output_part(3)
    s_first(1)
    dhidden_part(2, True)
    g_done(3)
    dhidden_part(3, False)
    backward()
    transpose(dgate, dgT)
    w_part(1)
    transpose(dup, duT)
    s_join(0)
    w_part(2)
    w_cross(1)
    s_join(1)
    input_part(0)
    input_part(1)
    w_cross(2)
    s_first(2)
    s_second(0)
    input_part(2)
    input_part(3)
    s_first(3)
    s_second(1)
    w_part(3)
    s_join(2)
    s_third(0)
    w_part(4)
    s_join(3)
    s_third(1)
    w_part(5)
    s_finish(0)
    s_finish(1)
    s_second(2)
    w_finish(0)
    s_second(3)
    s_third(2)
    s_third(3)
    s_finish(2)
    s_finish(3)
    w_finish(1)
    w_finish(2)
    for cp in started:
        cp.wait_send()
    for cp in stores:
        cp.wait()


def body(tokens, cotangent, gate_weight, up_weight, down_weight):
    any_spec = pl.BlockSpec(memory_space=pl.ANY)
    vm, dma = pltpu.VMEM, pltpu.SemaphoreType.DMA
    blocks = (4, 4, 32, Q)
    return pl.pallas_call(
        kernel,
        out_shape=(
            jax.ShapeDtypeStruct((16, D), BF16),
            jax.ShapeDtypeStruct((16, D), BF16),
            jax.ShapeDtypeStruct((Q, H), BF16),
            jax.ShapeDtypeStruct((Q, H), BF16),
            jax.ShapeDtypeStruct((H, Q), BF16),
        ),
        in_specs=[any_spec] * 5,
        out_specs=[any_spec] * 5,
        scratch_shapes=[
            vm((8,) + blocks, BF16),
            vm((D, H), BF16), vm((D, H), BF16), vm((4, H, Q), BF16),
            vm((T, H), F32), vm((T, H), F32), vm((T, H), F32),
            vm((T, H), BF16), vm((T, H), BF16), vm((T, H), BF16),
            vm((H, T), BF16), vm((H, T), BF16), vm((H, T), BF16),
            vm((8,) + blocks, BF16),
            vm((4, 2, 2, 4, 32, Q), BF16),
            vm((4, 2, 2, 4, 16, Q), BF16),
            vm((4, 2, 3, 32, Q), BF16),
            vm((4, 2, 16, Q), BF16), vm((4, 2, 16, Q), BF16),
            vm((4, 2, 16, Q), F32), vm((4, 2, 32, Q), F32),
            vm((2, 16, D), BF16),
            vm((8, H, Q), BF16), vm((6, H, Q), BF16), vm((3, H, Q), BF16),
            dma((19,)), dma((4, 45)), dma((4, 45)), dma((4, 19)), dma((4, 19)),
            dma((6,)), dma((6,)), dma((3,)), dma((3,)),
        ],
        compiler_params=pltpu.CompilerParams(
            collective_id=0, has_side_effects=True, vmem_limit_bytes=62 * 1024 * 1024
        ),
        cost_estimate=pl.CostEstimate(flops=17_000_000_000, bytes_accessed=15_000_000, transcendentals=460_000),
    )(tokens, cotangent, gate_weight, up_weight, down_weight)


def solution(mesh):
    placed = (
        P(("dp", "tensor"), None),
        P(("dp", "tensor"), None),
        P(None, "tensor"),
        P(None, "tensor"),
        P("tensor", None),
    )
    return jax.shard_map(
        body,
        mesh=mesh,
        in_specs=placed,
        out_specs=(
            P(("dp", "tensor"), None),
            P(("dp", "tensor"), None),
            P("dp", "tensor"),
            P("dp", "tensor"),
            P("tensor", "dp"),
        ),
        check_vma=False,
    )
```

```python
import jax
import jax.numpy as jnp
from jax import lax
from jax.experimental import pallas as pl
from jax.experimental.pallas import tpu as pltpu
from jax.sharding import PartitionSpec as P

MESH = pl.DeviceIdType.MESH
BF16, F32 = jnp.bfloat16, jnp.float32
T, D, H, Q = 512, 4096, 448, 1024


def mm(a, b):
    return jnp.dot(a, b, preferred_element_type=F32)


def mm_nt(a, b):
    return lax.dot_general(a, b, (((1,), (1,)), ((), ())), preferred_element_type=F32)


def kernel(
    tok, cot, wg, wu, wd,
    out, ig, gg, ug, dg,
    X, WG, WU, WD, gate, up, dhid, hid, dgate, dup, hidT, dgT, duT,
    PS, R1, RF, R2, R3, TS, TO, SO, OB, WB, CR, XR,
    ls, gs, gr, ss, sr, cs, cr, xs, xr,
):
    dp, t = lax.axis_index("dp"), lax.axis_index("tensor")
    xl, c = dp // 2, lax.rem(dp, 2)
    z, y, xh = t // 8, lax.rem(t // 2, 4), lax.rem(t, 2)

    def ring(v, off):
        return lax.rem(v + (off + 4) % 4, 4)

    def dev(zz, yy, hh=None):
        return (dp, zz * 8 + yy * 2 + (xh if hh is None else hh))

    x_pair = ((1 - xl) * 2 + c, t)
    core_pair = (xl * 2 + 1 - c, t)
    h_pair = dev(z, y, 1 - xh)
    my_row = pl.multiple_of(xh * 16, 16)
    pair_row = pl.multiple_of((1 - xh) * 16, 16)
    OFFS = (1, -1, 2)

    def at(h, a, b):
        return (b, a) if h == 0 else (a, b)

    me_a, me_b = (y, z), (z, y)

    def peer(h, da=0, db=0):
        return dev(*at(h, ring(me_a[h], da), ring(me_b[h], db)))

    started = []

    def send(src, dst, s, r, to):
        cp = pltpu.make_async_remote_copy(
            src_ref=src, dst_ref=dst, send_sem=s, recv_sem=r, device_id=to, device_id_type=MESH
        )
        cp.start()
        started.append(cp)
        return cp

    def arrived(ref, r):
        pltpu.make_async_copy(ref, ref, r).wait()

    loads = []
    for arr, ref in enumerate((tok, cot)):
        for q in range(4):
            cp = pltpu.make_async_copy(
                ref.at[:, pl.ds(q * Q, Q)], X.at[arr * 4 + q, z, y, pl.ds(my_row, 16)], ls.at[arr * 4 + q]
            )
            cp.start()
            loads.append(cp)
    wloads = []
    for i, (ref, dst) in enumerate(((wg, WG), (wu, WU), (wd, WD))):
        for q in range(4):
            wloads.append(pltpu.make_async_copy(ref.at[:, pl.ds(q * Q, Q)], dst.at[q], ls.at[8 + i * 4 + q]))
    for cp in wloads:
        cp.start()

    barrier = pltpu.get_barrier_semaphore()
    peers = [x_pair, core_pair, h_pair]
    for off in OFFS:
        peers += [dev(ring(z, off), y), dev(z, ring(y, off))]
    for p in peers:
        pl.semaphore_signal(barrier, inc=1, device_id=p, device_id_type=MESH)
    pl.semaphore_wait(barrier, len(peers))

    base = (0, 2, 4 + (1 - xl) * 2, 4 + (1 - xl) * 2, 4 + xl * 2)
    cols = (pl.ds(0, Q), pl.ds(0, Q), pl.ds(0, 512), pl.ds(512, 512), pl.ds(0, Q))

    def blk(u, h, a, b):
        return X.at[(base[u] + h,) + at(h, a, b) + (slice(None), cols[u])]

    def sub(u, h, a, b, row):
        return X.at[(base[u] + h,) + at(h, a, b) + (pl.ds(row, 16), cols[u])]

    def gsend(u, i, ref, to):
        send(ref, ref, gs.at[u, i], gr.at[u, i], to)

    def g_start(u):
        ref = X.at[pl.ds(base[u], 2), z, y, pl.ds(my_row, 16), cols[u]]
        gsend(u, 0, ref, h_pair)
        for s, off in enumerate(OFFS):
            for h in range(2):
                gsend(u, 1 + h * 6 + s, sub(u, h, me_a[h], me_b[h], my_row), peer(h, da=off))
        g_near(u, my_row, 13, 8)

    def g_near(u, row, i, step):
        for h in range(2):
            for d, off in enumerate((1, -1)):
                gsend(u, i + h * step + d, sub(u, h, me_a[h], me_b[h], row), peer(h, db=off))

    def g_spread(u, s):
        for h in range(2):
            a = ring(me_a[h], -OFFS[s - 1])
            for d, off in enumerate((1, -1)):
                gsend(u, 13 + h * 8 + s * 2 + d, blk(u, h, a, me_b[h]), peer(h, db=off))

    def g_own(u):
        arrived(X.at[pl.ds(base[u], 2), z, y, pl.ds(pair_row, 16), cols[u]], gr.at[u, 0])
        for s, off in enumerate(OFFS):
            for h in range(2):
                gsend(u, 4 + h * 6 + s, sub(u, h, me_a[h], me_b[h], pair_row), peer(h, da=off))
        g_near(u, pair_row, 45, 2)

    def g_mid(u):
        for s in (1, 2, 3):
            for h in range(2):
                a = ring(me_a[h], -OFFS[s - 1])
                arrived(sub(u, h, a, me_b[h], my_row), gr.at[u, 1 + h * 6 + s - 1])
                arrived(sub(u, h, a, me_b[h], pair_row), gr.at[u, 4 + h * 6 + s - 1])
            g_spread(u, s)

    def g_forward(u):
        for s in range(4):
            for h in range(2):
                a = me_a[h] if s == 0 else ring(me_a[h], -OFFS[s - 1])
                for d, off in enumerate((1, -1)):
                    b = ring(me_b[h], -off)
                    i = h * 8 + s * 2 + d
                    if s == 0:
                        arrived(sub(u, h, a, b, my_row), gr.at[u, 13 + i])
                        arrived(sub(u, h, a, b, pair_row), gr.at[u, 45 + h * 2 + d])
                    else:
                        arrived(blk(u, h, a, b), gr.at[u, 13 + i])
                    gsend(u, 29 + i, sub(u, h, a, b, d * 16), peer(h, db=off))

    def g_done(u):
        for s in range(4):
            for h in range(2):
                a = me_a[h] if s == 0 else ring(me_a[h], -OFFS[s - 1])
                for d in range(2):
                    arrived(sub(u, h, a, ring(me_b[h], 2), d * 16), gr.at[u, 29 + h * 8 + s * 2 + d])

    def rows_of(i, r):
        return X[i, pl.ds(2 * r, 2)].reshape(256, Q)

    def gate_up(w):
        for q in (2 * w, 2 * w + 1):
            def step(r, _):
                x = rows_of(q, r)
                rows = pl.ds(pl.multiple_of(r * 256, 256), 256)
                g = mm_nt(x, WG[q])
                u = mm_nt(x, WU[q])
                if q == 0:
                    gate[rows, :] = g
                    up[rows, :] = u
                else:
                    gate[rows, :] += g
                    up[rows, :] += u
                return 0

            lax.fori_loop(0, 2, step, 0)

    def hidden():
        def step(r, _):
            rows = pl.ds(pl.multiple_of(r * 32, 32), 32)
            g = gate[rows, :]
            hid[rows, :] = (g * jax.nn.sigmoid(g) * up[rows, :]).astype(BF16)
            return 0

        lax.fori_loop(0, 16, step, 0)

    def backward():
        def step(r, _):
            rows = pl.ds(pl.multiple_of(r * 32, 32), 32)
            g, dh = gate[rows, :], dhid[rows, :]
            sig = jax.nn.sigmoid(g)
            dgate[rows, :] = (dh * up[rows, :] * sig * (1.0 + g * (1.0 - sig))).astype(BF16)
            dup[rows, :] = (dh * (g * sig)).astype(BF16)
            return 0

        lax.fori_loop(0, 16, step, 0)

    def transpose(src, dst):
        for r in range(4):
            dst[:, r * 128:(r + 1) * 128] = src[r * 128:(r + 1) * 128, :].astype(F32).T.astype(BF16)

    def output_part(q):
        def step(r, _):
            rows = pl.ds(pl.multiple_of(r * 256, 256), 256)
            PS[q, pl.ds(2 * r, 2)] = mm(hid[rows, :], WD[q]).astype(BF16).reshape(2, 4, 32, Q)
            return 0

        lax.fori_loop(0, 2, step, 0)

    def dhidden_part(u, first):
        for h in range(2):
            def step(r, _):
                rows = pl.ds(pl.multiple_of(r * 256, 256), 256)
                x = X[base[u] + h, pl.ds(2 * r, 2), :, :, cols[u]]
                v = mm_nt(x.reshape(256, x.shape[-1]), WD[base[u] - 4 + h, :, cols[u]])
                if first and h == 0:
                    dhid[rows, :] = v
                else:
                    dhid[rows, :] += v
                return 0

            lax.fori_loop(0, 2, step, 0)

    def input_part(q):
        def step(r, _):
            rows = pl.ds(pl.multiple_of(r * 256, 256), 256)
            v = mm(dgate[rows, :], WG[q]) + mm(dup[rows, :], WU[q])
            PS[4 + q, pl.ds(2 * r, 2)] = v.astype(BF16).reshape(2, 4, 32, Q)
            return 0

        lax.fori_loop(0, 2, step, 0)

    def chunk(v, h, b, row, n):
        tail = (pl.ds(row, n), slice(None))
        i = (v // 2) * 4 + (v % 2) * 2 + h
        return (i, b, slice(None)) + tail if h == 0 else (i, slice(None), b) + tail

    def s_first(v):
        for h in range(2):
            for d, off in enumerate((1, -1)):
                k = h * 6 + d * 3
                far, near = ring(me_b[h], 2), ring(me_b[h], off)
                send(PS.at[chunk(v, h, far, d * 16, 16)], RF.at[v, h, d], ss.at[v, k], sr.at[v, k], peer(h, db=off))
                o = (1 - d) * 16
                send(
                    PS.at[chunk(v, h, near, o, 16)], R1.at[v, h, d, :, pl.ds(o, 16)],
                    ss.at[v, k + 1], sr.at[v, k + 1], peer(h, db=off),
                )

    def s_join(v):
        for h in range(2):
            for d, off in enumerate((1, -1)):
                k = h * 6 + d * 3
                near, o = ring(me_b[h], off), d * 16
                arrived(RF.at[v, h, d], sr.at[v, k])
                RF[v, h, d] = (
                    RF[v, h, d].astype(F32) + PS[chunk(v, h, near, o, 16)].astype(F32)
                ).astype(BF16)
                send(
                    RF.at[v, h, d], R1.at[v, h, d, :, pl.ds(o, 16)],
                    ss.at[v, k + 2], sr.at[v, k + 2], peer(h, db=off),
                )

    def s_second(v):
        for h in range(2):
            for d in range(2):
                k = h * 6 + d * 3
                arrived(R1.at[v, h, d, :, pl.ds((1 - d) * 16, 16)], sr.at[v, k + 1])
                arrived(R1.at[v, h, d, :, pl.ds(d * 16, 16)], sr.at[v, k + 2])
            i = (v // 2) * 4 + (v % 2) * 2 + h

            def total(a):
                own = PS[(i,) + at(h, a, me_b[h])].astype(F32)
                return own + R1[v, h, 0, a].astype(F32) + R1[v, h, 1, a].astype(F32)

            for s, off in enumerate(OFFS):
                a = ring(me_a[h], off)
                mine = (i,) + at(h, a, me_b[h])
                PS[mine] = total(a).astype(BF16)
                k = 12 + h * 3 + s
                send(PS.at[mine], R2.at[v, h, s], ss.at[v, k], sr.at[v, k], peer(h, da=off))
            SO[v, h] = total(me_a[h])

    def s_third(v):
        for h in range(2):
            for s in range(3):
                arrived(R2.at[v, h, s], sr.at[v, 12 + h * 3 + s])
            SO[v, h] = (
                SO[v, h] + R2[v, h, 0].astype(F32) + R2[v, h, 1].astype(F32) + R2[v, h, 2].astype(F32)
            )
            TO[v, h] = SO[v, h, pl.ds(my_row, 16)]
            TS[v, h] = SO[v, h, pl.ds(pair_row, 16)].astype(BF16)
        send(TS.at[v], R3.at[v], ss.at[v, 18], sr.at[v, 18], h_pair)

    stores = []

    def s_finish(v):
        arrived(R3.at[v], sr.at[v, 18])
        for h in range(2):
            q = (v % 2) * 2 + h
            OB[v // 2, :, q * Q:(q + 1) * Q] = (TO[v, h] + R3[v, h].astype(F32)).astype(BF16)
        if v % 2 == 1:
            cp = pltpu.make_async_copy(OB.at[v // 2], (out, ig)[v // 2], ls.at[20 + v // 2])
            cp.start()
            stores.append(cp)

    lhs, x0 = (hidT, dgT, duT), (4, 0, 0)
    jobs = {}

    def w_part(j, n):
        arr, w = j % 3, (1 - xl) if j < 3 else xl
        part = pl.ds(n * 512, 512)
        if j >= 2:
            old = jobs[j - 2, n]
            old.wait_send()
            started[:] = [cp for cp in started if cp is not old]

        def step(k, _):
            quarter = w * 2 + jnp.where(k == 0, 1 - c, c)
            slot = jnp.where(k == 0, 6 + j % 2, j)
            xb = X[x0[arr] + quarter, :, :, :, part].reshape(T, 512)
            WB[slot, :, part] = mm(lhs[arr][...], xb).astype(BF16)
            return 0

        lax.fori_loop(0, 2, step, 0)
        jobs[j, n] = send(
            WB.at[6 + j % 2, :, part], CR.at[j, :, part], cs.at[j, n], cr.at[j, n], core_pair
        )

    def w_cross(j, n):
        part = pl.ds(n * 512, 512)
        arrived(CR.at[j, :, part], cr.at[j, n])

        def step(r, _):
            rows = pl.ds(pl.multiple_of(r * 64, 64), 64)
            WB[j, rows, part] = (WB[j, rows, part].astype(F32) + CR[j, rows, part].astype(F32)).astype(BF16)
            return 0

        lax.fori_loop(0, 7, step, 0)
        send(WB.at[j, :, part], XR.at[j, :, part], xs.at[j, n], xr.at[j, n], x_pair)

    def w_finish(arr, n):
        j = 3 + arr
        part = pl.ds(n * 512, 512)
        arrived(CR.at[j, :, part], cr.at[j, n])
        arrived(XR.at[arr, :, part], xr.at[arr, n])

        def step(r, _):
            rows = pl.ds(pl.multiple_of(r * 64, 64), 64)
            v = WB[j, rows, part].astype(F32) + CR[j, rows, part].astype(F32) + XR[arr, rows, part].astype(F32)
            WB[j, rows, part] = v.astype(BF16)
            return 0

        lax.fori_loop(0, 7, step, 0)
        cp = pltpu.make_async_copy(WB.at[j, :, part], (dg, gg, ug)[arr].at[:, part], ls.at[22 + arr * 2 + n])
        cp.start()
        stores.append(cp)

    for cp in loads:
        cp.wait()
    g_start(0)
    g_start(1)
    g_own(0)
    g_own(1)
    g_mid(0)
    g_forward(0)
    g_start(2)
    g_mid(1)
    g_own(2)
    g_done(0)
    for cp in wloads:
        cp.wait()
    gate_up(0)
    g_forward(1)
    g_mid(2)
    g_start(3)
    g_done(1)
    g_own(3)
    gate_up(1)
    g_forward(2)
    g_mid(3)
    g_start(4)
    hidden()
    transpose(hid, hidT)
    g_done(2)
    w_part(0, 0)
    g_own(4)
    g_forward(3)
    w_cross(0, 0)
    g_mid(4)
    output_part(0)
    g_done(3)
    w_part(0, 1)
    output_part(1)
    w_cross(0, 1)
    g_forward(4)
    s_first(0)
    output_part(2)
    dhidden_part(2, True)
    dhidden_part(3, False)
    output_part(3)
    s_first(1)
    g_done(4)
    dhidden_part(4, False)
    backward()
    transpose(dgate, dgT)
    w_part(1, 0)
    w_part(1, 1)
    w_cross(1, 0)
    transpose(dup, duT)
    w_cross(1, 1)
    s_join(0)
    w_part(2, 0)
    w_part(2, 1)
    w_cross(2, 0)
    s_join(1)
    w_cross(2, 1)
    input_part(0)
    input_part(1)
    s_first(2)
    s_second(0)
    input_part(2)
    input_part(3)
    s_first(3)
    s_second(1)
    s_join(2)
    w_part(3, 0)
    w_part(3, 1)
    s_third(0)
    s_join(3)
    s_third(1)
    w_part(4, 0)
    w_part(4, 1)
    s_second(2)
    w_part(5, 0)
    w_part(5, 1)
    s_second(3)
    w_finish(0, 0)
    w_finish(0, 1)
    s_third(2)
    s_third(3)
    s_finish(0)
    s_finish(1)
    w_finish(1, 0)
    w_finish(1, 1)
    s_finish(2)
    s_finish(3)
    w_finish(2, 0)
    w_finish(2, 1)
    for cp in started:
        cp.wait_send()
    for cp in stores:
        cp.wait()


def store(*refs):
    sems = refs[15]
    into = [pltpu.make_async_copy(refs[i], refs[10 + i], sems.at[i]) for i in range(5)]
    back = [pltpu.make_async_copy(refs[10 + i], refs[5 + i], sems.at[5 + i]) for i in range(5)]
    for cp in into:
        cp.start()
    for a, b in zip(into, back):
        a.wait()
        b.start()
    for cp in back:
        cp.wait()


def body(tokens, cotangent, gate_weight, up_weight, down_weight):
    any_spec = pl.BlockSpec(memory_space=pl.ANY)
    vm, dma = pltpu.VMEM, pltpu.SemaphoreType.DMA
    blocks = (4, 4, 32, Q)
    shapes = [jax.ShapeDtypeStruct((16, D), BF16)] * 2 + [jax.ShapeDtypeStruct((H, Q), BF16)] * 3
    results = pl.pallas_call(
        kernel,
        out_shape=shapes,
        in_specs=[any_spec] * 5,
        out_specs=[any_spec] * 5,
        scratch_shapes=[
            vm((8,) + blocks, BF16),
            vm((4, H, Q), BF16), vm((4, H, Q), BF16), vm((4, H, Q), BF16),
            vm((T, H), F32), vm((T, H), F32), vm((T, H), F32),
            vm((T, H), BF16), vm((T, H), BF16), vm((T, H), BF16),
            vm((H, T), BF16), vm((H, T), BF16), vm((H, T), BF16),
            vm((8,) + blocks, BF16),
            vm((4, 2, 2, 4, 32, Q), BF16),
            vm((4, 2, 2, 4, 16, Q), BF16),
            vm((4, 2, 3, 32, Q), BF16),
            vm((4, 2, 16, Q), BF16), vm((4, 2, 16, Q), BF16),
            vm((4, 2, 16, Q), F32), vm((4, 2, 32, Q), F32),
            vm((2, 16, D), BF16),
            vm((8, H, Q), BF16), vm((6, H, Q), BF16), vm((3, H, Q), BF16),
            dma((28,)), dma((5, 49)), dma((5, 49)), dma((4, 19)), dma((4, 19)),
            dma((6, 2)), dma((6, 2)), dma((3, 2)), dma((3, 2)),
        ],
        compiler_params=pltpu.CompilerParams(
            collective_id=0, has_side_effects=True, vmem_limit_bytes=62 * 1024 * 1024
        ),
        cost_estimate=pl.CostEstimate(flops=17_000_000_000, bytes_accessed=15_000_000, transcendentals=460_000),
    )(tokens, cotangent, gate_weight.T, up_weight.T, down_weight)
    output, input_grad, gate_grad, up_grad, down_grad = pl.pallas_call(
        store,
        out_shape=shapes,
        in_specs=[any_spec] * 5,
        out_specs=[any_spec] * 5,
        scratch_shapes=[vm(x.shape, BF16) for x in shapes] + [dma((10,))],
    )(*results)
    return output, input_grad, gate_grad.T, up_grad.T, down_grad


def solution(mesh):
    placed = (
        P(("dp", "tensor"), None),
        P(("dp", "tensor"), None),
        P(None, "tensor"),
        P(None, "tensor"),
        P("tensor", None),
    )
    return jax.shard_map(
        body,
        mesh=mesh,
        in_specs=placed,
        out_specs=(
            P(("dp", "tensor"), None),
            P(("dp", "tensor"), None),
            P("dp", "tensor"),
            P("dp", "tensor"),
            P("tensor", "dp"),
        ),
        check_vma=False,
    )
```

```python
import jax
import jax.numpy as jnp
from jax import lax
from jax.experimental import pallas as pl
from jax.experimental.pallas import tpu as pltpu
from jax.sharding import PartitionSpec as P

MESH = pl.DeviceIdType.MESH
BF16, F32 = jnp.bfloat16, jnp.float32
T, D, H, Q = 512, 4096, 448, 1024


def mm(a, b):
    return jnp.dot(a, b, preferred_element_type=F32)


def mm_nt(a, b):
    return lax.dot_general(a, b, (((1,), (1,)), ((), ())), preferred_element_type=F32)


def kernel(
    tok, cot, wg, wu, wd,
    out, ig, gg, ug, dg,
    X, WG, WU, WD, gate, up, dhid, hid, dgate, dup, hidT, dgT, duT,
    PS, R1, RF, R2, R3, TS, TO, SO, OB, WB, CR, XR,
    ls, gs, gr, ss, sr, cs, cr, xs, xr,
):
    dp, t = lax.axis_index("dp"), lax.axis_index("tensor")
    xl, c = dp // 2, lax.rem(dp, 2)
    z, y, xh = t // 8, lax.rem(t // 2, 4), lax.rem(t, 2)

    def ring(v, off):
        return lax.rem(v + (off + 4) % 4, 4)

    def dev(zz, yy, hh=None):
        return (dp, zz * 8 + yy * 2 + (xh if hh is None else hh))

    x_pair = ((1 - xl) * 2 + c, t)
    core_pair = (xl * 2 + 1 - c, t)
    h_pair = dev(z, y, 1 - xh)
    my_row = pl.multiple_of(xh * 16, 16)
    pair_row = pl.multiple_of((1 - xh) * 16, 16)
    OFFS = (1, -1, 2)

    def at(h, a, b):
        return (b, a) if h == 0 else (a, b)

    me_a, me_b = (y, z), (z, y)

    def peer(h, da=0, db=0):
        return dev(*at(h, ring(me_a[h], da), ring(me_b[h], db)))

    started = []

    def send(src, dst, s, r, to):
        cp = pltpu.make_async_remote_copy(
            src_ref=src, dst_ref=dst, send_sem=s, recv_sem=r, device_id=to, device_id_type=MESH
        )
        cp.start()
        started.append(cp)
        return cp

    def arrived(ref, r):
        pltpu.make_async_copy(ref, ref, r).wait()

    barrier = pltpu.get_barrier_semaphore()
    peers = [x_pair, core_pair, h_pair]
    for off in OFFS:
        peers += [dev(ring(z, off), y), dev(z, ring(y, off))]
    for p in peers:
        pl.semaphore_signal(barrier, inc=1, device_id=p, device_id_type=MESH)

    loads = []
    for arr, ref in enumerate((tok, cot)):
        for q in range(4):
            cp = pltpu.make_async_copy(
                ref.at[:, pl.ds(q * Q, Q)], X.at[arr * 4 + q, z, y, pl.ds(my_row, 16)], ls.at[arr * 4 + q]
            )
            cp.start()
            loads.append(cp)
    wloads = []
    for i, (ref, dst) in enumerate(((wg, WG), (wu, WU), (wd, WD))):
        for q in range(4):
            wloads.append(pltpu.make_async_copy(ref.at[:, pl.ds(q * Q, Q)], dst.at[q], ls.at[8 + i * 4 + q]))
    for cp in wloads:
        cp.start()

    pl.semaphore_wait(barrier, len(peers))

    base = (0, 2, 4 + (1 - xl) * 2, 4 + (1 - xl) * 2, 4 + xl * 2)
    cols = (pl.ds(0, Q), pl.ds(0, Q), pl.ds(0, 512), pl.ds(512, 512), pl.ds(0, Q))

    def blk(u, h, a, b):
        return X.at[(base[u] + h,) + at(h, a, b) + (slice(None), cols[u])]

    def sub(u, h, a, b, row):
        return X.at[(base[u] + h,) + at(h, a, b) + (pl.ds(row, 16), cols[u])]

    def gsend(u, i, ref, to):
        send(ref, ref, gs.at[u, i], gr.at[u, i], to)

    LATE = (0,)

    def g_pair(u):
        gsend(u, 0, X.at[pl.ds(base[u], 2), z, y, pl.ds(my_row, 16), cols[u]], h_pair)

    def g_start(u):
        for s, off in enumerate(OFFS):
            for h in range(2):
                gsend(u, 1 + h * 6 + s, sub(u, h, me_a[h], me_b[h], my_row), peer(h, da=off))
        g_near(u, my_row, 13, 8)

    def g_near(u, row, i, step):
        for h in range(2):
            for d, off in enumerate((1, -1)):
                gsend(u, i + h * step + d, sub(u, h, me_a[h], me_b[h], row), peer(h, db=off))

    def g_own(u):
        arrived(X.at[pl.ds(base[u], 2), z, y, pl.ds(pair_row, 16), cols[u]], gr.at[u, 0])
        for s, off in enumerate(OFFS):
            for h in range(2):
                gsend(u, 4 + h * 6 + s, sub(u, h, me_a[h], me_b[h], pair_row), peer(h, da=off))
        g_near(u, pair_row, 45, 2)

    def g_part(u, h, s, b):
        a = me_a[h] if s == 0 else ring(me_a[h], -OFFS[s - 1])
        return sub(u, h, a, b, my_row) if u in LATE else blk(u, h, a, b)

    def g_mid(u):
        for s in (1, 2, 3):
            for h in range(2):
                a = ring(me_a[h], -OFFS[s - 1])
                mine = sub(u, h, a, me_b[h], my_row)
                arrived(mine, gr.at[u, s + h * 6])
                if u not in LATE:
                    arrived(sub(u, h, a, me_b[h], pair_row), gr.at[u, 3 + s + h * 6])
                for d, off in enumerate((1, -1)):
                    gsend(u, 13 + h * 8 + s * 2 + d, g_part(u, h, s, me_b[h]), peer(h, db=off))
        if u in LATE:
            g_swap(u, 0)

    def plane(u, h, b, row):
        tail = (pl.ds(row, 16), cols[u])
        i = base[u] + h
        return X.at[(i, b, slice(None)) + tail] if h == 0 else X.at[(i, slice(None), b) + tail]

    def g_swap(u, stage):
        for h in range(2):
            for k in ((0,), (1, 2), (3,))[stage]:
                gsend(u, 45 + h * 4 + k, plane(u, h, ring(me_b[h], (0, 1, -1, 2)[k]), my_row), h_pair)

    def g_forward(u):
        for s in range(4):
            for h in range(2):
                for d, off in enumerate((1, -1)):
                    b = ring(me_b[h], -off)
                    i = h * 8 + s * 2 + d
                    if s == 0 and u not in LATE:
                        arrived(sub(u, h, me_a[h], b, my_row), gr.at[u, 13 + i])
                        arrived(sub(u, h, me_a[h], b, pair_row), gr.at[u, 45 + h * 2 + d])
                    else:
                        arrived(g_part(u, h, s, b), gr.at[u, 13 + i])
                    if u not in LATE:
                        a = me_a[h] if s == 0 else ring(me_a[h], -OFFS[s - 1])
                        gsend(u, 29 + i, sub(u, h, a, b, d * 16), peer(h, db=off))
                    elif s // 2 == d:
                        gsend(u, 29 + i, g_part(u, h, s, b), peer(h, db=off))
        if u in LATE:
            g_swap(u, 1)

    def g_done(u):
        for s in range(4):
            for h in range(2):
                b = ring(me_b[h], 2)
                for d in range(2):
                    i = 29 + h * 8 + s * 2 + d
                    if u not in LATE:
                        a = me_a[h] if s == 0 else ring(me_a[h], -OFFS[s - 1])
                        arrived(sub(u, h, a, b, d * 16), gr.at[u, i])
                    elif s // 2 == d:
                        arrived(g_part(u, h, s, b), gr.at[u, i])
        if u in LATE:
            g_swap(u, 2)

    def g_swapped(u):
        for h in range(2):
            for k in range(4):
                arrived(plane(u, h, ring(me_b[h], (0, 1, -1, 2)[k]), pair_row), gr.at[u, 45 + h * 4 + k])

    def rows_of(i, r):
        return X[i, pl.ds(2 * r, 2)].reshape(256, Q)

    def gate_up(w):
        for q in (2 * w, 2 * w + 1):
            def step(r, _):
                x = rows_of(q, r)
                rows = pl.ds(pl.multiple_of(r * 256, 256), 256)
                g = mm_nt(x, WG[q])
                u = mm_nt(x, WU[q])
                if q == 2:
                    gate[rows, :] = g
                    up[rows, :] = u
                else:
                    gate[rows, :] += g
                    up[rows, :] += u
                return 0

            lax.fori_loop(0, 2, step, 0)

    def hidden():
        def step(r, _):
            rows = pl.ds(pl.multiple_of(r * 32, 32), 32)
            g = gate[rows, :]
            hid[rows, :] = (g * jax.nn.sigmoid(g) * up[rows, :]).astype(BF16)
            return 0

        lax.fori_loop(0, 16, step, 0)

    def factors():
        def step(r, _):
            rows = pl.ds(pl.multiple_of(r * 32, 32), 32)
            g = gate[rows, :]
            sig = jax.nn.sigmoid(g)
            gate[rows, :] = up[rows, :] * sig * (1.0 + g * (1.0 - sig))
            up[rows, :] = g * sig
            return 0

        lax.fori_loop(0, 16, step, 0)

    def backward(dst, factor):
        def step(r, _):
            rows = pl.ds(pl.multiple_of(r * 64, 64), 64)
            dst[rows, :] = (dhid[rows, :] * factor[rows, :]).astype(BF16)
            return 0

        lax.fori_loop(0, 8, step, 0)

    def transpose(src, dst):
        for r in range(4):
            dst[:, r * 128:(r + 1) * 128] = src[r * 128:(r + 1) * 128, :].astype(F32).T.astype(BF16)

    def output_part(q):
        def step(r, _):
            rows = pl.ds(pl.multiple_of(r * 256, 256), 256)
            PS[q, pl.ds(2 * r, 2)] = mm(hid[rows, :], WD[q]).astype(BF16).reshape(2, 4, 32, Q)
            return 0

        lax.fori_loop(0, 2, step, 0)

    def dhidden_part(u, first):
        for h in range(2):
            def step(r, _):
                rows = pl.ds(pl.multiple_of(r * 256, 256), 256)
                x = X[base[u] + h, pl.ds(2 * r, 2), :, :, cols[u]]
                v = mm_nt(x.reshape(256, x.shape[-1]), WD[base[u] - 4 + h, :, cols[u]])
                if first and h == 0:
                    dhid[rows, :] = v
                else:
                    dhid[rows, :] += v
                return 0

            lax.fori_loop(0, 2, step, 0)

    def input_part(q):
        def step(r, _):
            rows = pl.ds(pl.multiple_of(r * 256, 256), 256)
            v = mm(dgate[rows, :], WG[q]) + mm(dup[rows, :], WU[q])
            PS[4 + q, pl.ds(2 * r, 2)] = v.astype(BF16).reshape(2, 4, 32, Q)
            return 0

        lax.fori_loop(0, 2, step, 0)

    def chunk(v, h, b, row, n):
        tail = (pl.ds(row, n), slice(None))
        i = (v // 2) * 4 + (v % 2) * 2 + h
        return (i, b, slice(None)) + tail if h == 0 else (i, slice(None), b) + tail

    def s_first(v):
        for h in range(2):
            for d, off in enumerate((1, -1)):
                k = h * 6 + d * 3
                far, near = ring(me_b[h], 2), ring(me_b[h], off)
                send(PS.at[chunk(v, h, far, d * 16, 16)], RF.at[v, h, d], ss.at[v, k], sr.at[v, k], peer(h, db=off))
                o = (1 - d) * 16
                send(
                    PS.at[chunk(v, h, near, o, 16)], R1.at[v, h, d, :, pl.ds(o, 16)],
                    ss.at[v, k + 1], sr.at[v, k + 1], peer(h, db=off),
                )

    def s_join(v):
        for h in range(2):
            for d, off in enumerate((1, -1)):
                k = h * 6 + d * 3
                near, o = ring(me_b[h], off), d * 16
                arrived(RF.at[v, h, d], sr.at[v, k])
                RF[v, h, d] = (
                    RF[v, h, d].astype(F32) + PS[chunk(v, h, near, o, 16)].astype(F32)
                ).astype(BF16)
                send(
                    RF.at[v, h, d], R1.at[v, h, d, :, pl.ds(o, 16)],
                    ss.at[v, k + 2], sr.at[v, k + 2], peer(h, db=off),
                )

    def s_second(v):
        for h in range(2):
            for d in range(2):
                k = h * 6 + d * 3
                arrived(R1.at[v, h, d, :, pl.ds((1 - d) * 16, 16)], sr.at[v, k + 1])
                arrived(R1.at[v, h, d, :, pl.ds(d * 16, 16)], sr.at[v, k + 2])
            i = (v // 2) * 4 + (v % 2) * 2 + h

            def total(a):
                own = PS[(i,) + at(h, a, me_b[h])].astype(F32)
                return own + R1[v, h, 0, a].astype(F32) + R1[v, h, 1, a].astype(F32)

            for s, off in enumerate(OFFS):
                a = ring(me_a[h], off)
                mine = (i,) + at(h, a, me_b[h])
                PS[mine] = total(a).astype(BF16)
                k = 12 + h * 3 + s
                send(PS.at[mine], R2.at[v, h, s], ss.at[v, k], sr.at[v, k], peer(h, da=off))
            SO[v, h] = total(me_a[h])

    def s_third(v):
        for h in range(2):
            for s in range(3):
                arrived(R2.at[v, h, s], sr.at[v, 12 + h * 3 + s])
            SO[v, h] = (
                SO[v, h] + R2[v, h, 0].astype(F32) + R2[v, h, 1].astype(F32) + R2[v, h, 2].astype(F32)
            )
            TO[v, h] = SO[v, h, pl.ds(my_row, 16)]
            TS[v, h] = SO[v, h, pl.ds(pair_row, 16)].astype(BF16)
        send(TS.at[v], R3.at[v], ss.at[v, 18], sr.at[v, 18], h_pair)

    stores = []

    def s_finish(v):
        arrived(R3.at[v], sr.at[v, 18])
        for h in range(2):
            q = (v % 2) * 2 + h
            OB[v // 2, :, q * Q:(q + 1) * Q] = (TO[v, h] + R3[v, h].astype(F32)).astype(BF16)
        if v % 2 == 1:
            cp = pltpu.make_async_copy(OB.at[v // 2], (out, ig)[v // 2], ls.at[20 + v // 2])
            cp.start()
            stores.append(cp)

    lhs, x0 = (hidT, dgT, duT), (4, 0, 0)
    jobs = {}

    def w_part(j, n):
        arr, w = j % 3, (1 - xl) if j < 3 else xl
        part = pl.ds(n * 512, 512)
        if j >= 2:
            old = jobs[j - 2, n]
            old.wait_send()
            started[:] = [cp for cp in started if cp is not old]

        def step(k, _):
            quarter = w * 2 + jnp.where(k == 0, 1 - c, c)
            slot = jnp.where(k == 0, 6 + j % 2, j)
            xb = X[x0[arr] + quarter, :, :, :, part].reshape(T, 512)
            WB[slot, :, part] = mm(lhs[arr][...], xb).astype(BF16)
            return 0

        lax.fori_loop(0, 2, step, 0)
        jobs[j, n] = send(
            WB.at[6 + j % 2, :, part], CR.at[j, :, part], cs.at[j, n], cr.at[j, n], core_pair
        )

    def w_cross(j, n):
        part = pl.ds(n * 512, 512)
        arrived(CR.at[j, :, part], cr.at[j, n])

        def step(r, _):
            rows = pl.ds(pl.multiple_of(r * 64, 64), 64)
            WB[j, rows, part] = (WB[j, rows, part].astype(F32) + CR[j, rows, part].astype(F32)).astype(BF16)
            return 0

        lax.fori_loop(0, 7, step, 0)
        send(WB.at[j, :, part], XR.at[j, :, part], xs.at[j, n], xr.at[j, n], x_pair)

    def w_finish(arr, n):
        j = 3 + arr
        part = pl.ds(n * 512, 512)
        arrived(CR.at[j, :, part], cr.at[j, n])
        arrived(XR.at[arr, :, part], xr.at[arr, n])

        def step(r, _):
            rows = pl.ds(pl.multiple_of(r * 64, 64), 64)
            v = WB[j, rows, part].astype(F32) + CR[j, rows, part].astype(F32) + XR[arr, rows, part].astype(F32)
            WB[j, rows, part] = v.astype(BF16)
            return 0

        lax.fori_loop(0, 7, step, 0)
        cp = pltpu.make_async_copy(WB.at[j, :, part], (dg, gg, ug)[arr].at[:, part], ls.at[22 + arr * 2 + n])
        cp.start()
        stores.append(cp)

    for cp in loads:
        cp.wait()
    g_pair(1)
    g_start(0)
    g_start(1)
    g_pair(2)
    g_pair(3)
    g_pair(4)
    g_own(1)
    g_mid(0)
    g_forward(0)
    g_start(2)
    g_mid(1)
    g_own(2)
    g_done(0)
    for cp in wloads:
        cp.wait()
    g_forward(1)
    g_mid(2)
    g_start(3)
    g_done(1)
    g_own(3)
    gate_up(1)
    g_forward(2)
    g_mid(3)
    g_start(4)
    g_swapped(0)
    gate_up(0)
    hidden()
    transpose(hid, hidT)
    g_done(2)
    w_part(0, 0)
    g_own(4)
    g_forward(3)
    w_cross(0, 0)
    g_mid(4)
    output_part(0)
    g_done(3)
    w_part(0, 1)
    output_part(1)
    w_cross(0, 1)
    factors()
    g_forward(4)
    s_first(0)
    output_part(2)
    dhidden_part(2, True)
    dhidden_part(3, False)
    output_part(3)
    s_first(1)
    g_done(4)
    dhidden_part(4, False)
    backward(dgate, gate)
    transpose(dgate, dgT)
    w_part(1, 0)
    w_part(1, 1)
    backward(dup, up)
    w_cross(1, 0)
    w_cross(1, 1)
    s_join(0)
    input_part(0)
    input_part(1)
    s_first(2)
    transpose(dup, duT)
    w_part(2, 0)
    s_join(1)
    w_part(2, 1)
    w_cross(2, 0)
    s_second(0)
    input_part(2)
    input_part(3)
    s_first(3)
    s_second(1)
    s_join(2)
    s_third(0)
    w_part(3, 0)
    w_part(3, 1)
    s_join(3)
    s_third(1)
    w_cross(2, 1)
    w_part(4, 0)
    w_part(4, 1)
    s_second(2)
    w_part(5, 0)
    w_part(5, 1)
    w_finish(0, 0)
    w_finish(0, 1)
    s_third(2)
    s_second(3)
    s_finish(0)
    s_finish(1)
    w_finish(1, 0)
    s_third(3)
    w_finish(1, 1)
    s_finish(2)
    w_finish(2, 0)
    s_finish(3)
    w_finish(2, 1)
    for cp in started:
        cp.wait_send()
    for cp in stores:
        cp.wait()


def store(*refs):
    sems = refs[15]
    into = [pltpu.make_async_copy(refs[i], refs[10 + i], sems.at[i]) for i in range(5)]
    back = [pltpu.make_async_copy(refs[10 + i], refs[5 + i], sems.at[5 + i]) for i in range(5)]
    for cp in into:
        cp.start()
    for a, b in zip(into, back):
        a.wait()
        b.start()
    for cp in back:
        cp.wait()


def body(tokens, cotangent, gate_weight, up_weight, down_weight):
    any_spec = pl.BlockSpec(memory_space=pl.ANY)
    vm, dma = pltpu.VMEM, pltpu.SemaphoreType.DMA
    blocks = (4, 4, 32, Q)
    shapes = [jax.ShapeDtypeStruct((16, D), BF16)] * 2 + [jax.ShapeDtypeStruct((H, Q), BF16)] * 3
    results = pl.pallas_call(
        kernel,
        out_shape=shapes,
        in_specs=[any_spec] * 5,
        out_specs=[any_spec] * 5,
        scratch_shapes=[
            vm((8,) + blocks, BF16),
            vm((4, H, Q), BF16), vm((4, H, Q), BF16), vm((4, H, Q), BF16),
            vm((T, H), F32), vm((T, H), F32), vm((T, H), F32),
            vm((T, H), BF16), vm((T, H), BF16), vm((T, H), BF16),
            vm((H, T), BF16), vm((H, T), BF16), vm((H, T), BF16),
            vm((8,) + blocks, BF16),
            vm((4, 2, 2, 4, 32, Q), BF16),
            vm((4, 2, 2, 4, 16, Q), BF16),
            vm((4, 2, 3, 32, Q), BF16),
            vm((4, 2, 16, Q), BF16), vm((4, 2, 16, Q), BF16),
            vm((4, 2, 16, Q), F32), vm((4, 2, 32, Q), F32),
            vm((2, 16, D), BF16),
            vm((8, H, Q), BF16), vm((6, H, Q), BF16), vm((3, H, Q), BF16),
            dma((28,)), dma((5, 53)), dma((5, 53)), dma((4, 19)), dma((4, 19)),
            dma((6, 2)), dma((6, 2)), dma((3, 2)), dma((3, 2)),
        ],
        compiler_params=pltpu.CompilerParams(
            collective_id=0, has_side_effects=True, vmem_limit_bytes=62 * 1024 * 1024
        ),
        cost_estimate=pl.CostEstimate(flops=17_000_000_000, bytes_accessed=15_000_000, transcendentals=460_000),
    )(tokens, cotangent, gate_weight.T, up_weight.T, down_weight)
    output, input_grad, gate_grad, up_grad, down_grad = pl.pallas_call(
        store,
        out_shape=shapes,
        in_specs=[any_spec] * 5,
        out_specs=[any_spec] * 5,
        scratch_shapes=[vm(x.shape, BF16) for x in shapes] + [dma((10,))],
    )(*results)
    return output, input_grad, gate_grad.T, up_grad.T, down_grad


def solution(mesh):
    placed = (
        P(("dp", "tensor"), None),
        P(("dp", "tensor"), None),
        P(None, "tensor"),
        P(None, "tensor"),
        P("tensor", None),
    )
    return jax.shard_map(
        body,
        mesh=mesh,
        in_specs=placed,
        out_specs=(
            P(("dp", "tensor"), None),
            P(("dp", "tensor"), None),
            P("dp", "tensor"),
            P("dp", "tensor"),
            P("tensor", "dp"),
        ),
        check_vma=False,
    )
```

```python
import jax
import jax.numpy as jnp
from jax import lax
from jax.experimental import pallas as pl
from jax.experimental.pallas import tpu as pltpu
from jax.sharding import PartitionSpec as P

MESH = pl.DeviceIdType.MESH
BF16, F32 = jnp.bfloat16, jnp.float32
T, D, H, Q = 512, 4096, 448, 1024
PARTS = (pl.ds(0, 512), pl.ds(512, 512))


def mm(a, b):
    return jnp.dot(a, b, preferred_element_type=F32)


def mm_nt(a, b):
    return lax.dot_general(a, b, (((1,), (1,)), ((), ())), preferred_element_type=F32)


def kernel(
    tok, cot, wg, wu, wd,
    out, ig, gg, ug, dg,
    X, WG, WU, WD, gate, up, dhid, hid, dgate, dup, hidT, dgT, duT,
    PS, R1, RF, R2, R3, TS, TO, SO, OB, WB, CR, XR,
    ls, gs, gr, ss, sr, cs, cr, xs, xr,
):
    dp, t = lax.axis_index("dp"), lax.axis_index("tensor")
    xl, c = dp // 2, lax.rem(dp, 2)
    z, y, xh = t // 8, lax.rem(t // 2, 4), lax.rem(t, 2)

    def ring(v, off):
        return lax.rem(v + (off + 4) % 4, 4)

    def dev(zz, yy, hh=None):
        return (dp, zz * 8 + yy * 2 + (xh if hh is None else hh))

    x_pair = ((1 - xl) * 2 + c, t)
    core_pair = (xl * 2 + 1 - c, t)
    h_pair = dev(z, y, 1 - xh)
    my_row = pl.multiple_of(xh * 16, 16)
    pair_row = pl.multiple_of((1 - xh) * 16, 16)
    OFFS = (1, -1, 2)

    def at(h, a, b):
        return (b, a) if h == 0 else (a, b)

    me_a, me_b = (y, z), (z, y)

    def peer(h, da=0, db=0):
        return dev(*at(h, ring(me_a[h], da), ring(me_b[h], db)))

    started = []

    def send(src, dst, s, r, to):
        cp = pltpu.make_async_remote_copy(
            src_ref=src, dst_ref=dst, send_sem=s, recv_sem=r, device_id=to, device_id_type=MESH
        )
        cp.start()
        started.append(cp)
        return cp

    def arrived(ref, r):
        pltpu.make_async_copy(ref, ref, r).wait()

    barrier = pltpu.get_barrier_semaphore()
    peers = [x_pair, core_pair, h_pair]
    for off in OFFS:
        peers += [dev(ring(z, off), y), dev(z, ring(y, off))]
    for p in peers:
        pl.semaphore_signal(barrier, inc=1, device_id=p, device_id_type=MESH)

    loads = []
    for arr, ref in enumerate((tok, cot)):
        for q in range(4):
            cp = pltpu.make_async_copy(
                ref.at[:, pl.ds(q * Q, Q)], X.at[arr * 4 + q, z, y, pl.ds(my_row, 16)], ls.at[arr * 4 + q]
            )
            cp.start()
            loads.append(cp)
    wloads = []
    for i, (ref, dst) in enumerate(((wg, WG), (wu, WU), (wd, WD))):
        for q in range(4):
            wloads.append(pltpu.make_async_copy(ref.at[:, pl.ds(q * Q, Q)], dst.at[q], ls.at[8 + i * 4 + q]))
    for cp in wloads:
        cp.start()

    pl.semaphore_wait(barrier, len(peers))

    base = (0, 2, 4 + (1 - xl) * 2, 4 + (1 - xl) * 2, 4 + xl * 2)
    cols = (pl.ds(0, Q), pl.ds(0, Q), *PARTS, pl.ds(0, Q))

    def blk(u, h, a, b):
        return X.at[(base[u] + h,) + at(h, a, b) + (slice(None), cols[u])]

    def sub(u, h, a, b, row):
        return X.at[(base[u] + h,) + at(h, a, b) + (pl.ds(row, 16), cols[u])]

    def gsend(u, i, ref, to):
        send(ref, ref, gs.at[u, i], gr.at[u, i], to)

    LATE = (0,)
    RELAY = (1,)

    def g_pair(u):
        gsend(u, 0, X.at[pl.ds(base[u], 2), z, y, pl.ds(my_row, 16), cols[u]], h_pair)

    def g_start(u):
        for s, off in enumerate(OFFS[:2] if u in RELAY else OFFS):
            for h in range(2):
                gsend(u, 1 + h * 6 + s, sub(u, h, me_a[h], me_b[h], my_row), peer(h, da=off))
        g_near(u, my_row, 13, 8)

    def g_near(u, row, i, step):
        for h in range(2):
            for d, off in enumerate((1, -1)):
                gsend(u, i + h * step + d, sub(u, h, me_a[h], me_b[h], row), peer(h, db=off))

    def g_own(u):
        arrived(X.at[pl.ds(base[u], 2), z, y, pl.ds(pair_row, 16), cols[u]], gr.at[u, 0])
        for s, off in enumerate(OFFS[:2] if u in RELAY else OFFS):
            for h in range(2):
                gsend(u, 4 + h * 6 + s, sub(u, h, me_a[h], me_b[h], pair_row), peer(h, da=off))
        g_near(u, pair_row, 45, 2)

    def g_relay(u):
        for h in range(2):
            low, high = ring(me_a[h], -1), ring(me_a[h], 1)
            ref = sub(u, h, low, me_b[h], my_row)
            arrived(ref, gr.at[u, 1 + h * 6])
            gsend(u, 3 + h * 6, ref, peer(h, da=1))
            ref = sub(u, h, high, me_b[h], pair_row)
            arrived(ref, gr.at[u, 5 + h * 6])
            gsend(u, 6 + h * 6, ref, peer(h, da=-1))

    def g_part(u, h, s, b):
        a = me_a[h] if s == 0 else ring(me_a[h], -OFFS[s - 1])
        return sub(u, h, a, b, my_row) if u in LATE else blk(u, h, a, b)

    def g_mid(u, sides=(1, 2, 3)):
        for s in sides:
            for h in range(2):
                a = ring(me_a[h], -OFFS[s - 1])
                mine = sub(u, h, a, me_b[h], my_row)
                if u not in RELAY or s != 1:
                    arrived(mine, gr.at[u, s + h * 6])
                if u not in LATE and (u not in RELAY or s != 2):
                    arrived(sub(u, h, a, me_b[h], pair_row), gr.at[u, 3 + s + h * 6])
                for d, off in enumerate((1, -1)):
                    gsend(u, 13 + h * 8 + s * 2 + d, g_part(u, h, s, me_b[h]), peer(h, db=off))
        if u in LATE:
            g_swap(u, 0)

    def plane(u, h, b, row):
        tail = (pl.ds(row, 16), cols[u])
        i = base[u] + h
        return X.at[(i, b, slice(None)) + tail] if h == 0 else X.at[(i, slice(None), b) + tail]

    def g_swap(u, stage):
        for h in range(2):
            for k in ((0,), (1, 2), (3,))[stage]:
                gsend(u, 45 + h * 4 + k, plane(u, h, ring(me_b[h], (0, 1, -1, 2)[k]), my_row), h_pair)

    def g_forward(u):
        for s in range(4):
            for h in range(2):
                for d, off in enumerate((1, -1)):
                    b = ring(me_b[h], -off)
                    i = h * 8 + s * 2 + d
                    if s == 0 and u not in LATE:
                        arrived(sub(u, h, me_a[h], b, my_row), gr.at[u, 13 + i])
                        arrived(sub(u, h, me_a[h], b, pair_row), gr.at[u, 45 + h * 2 + d])
                    else:
                        arrived(g_part(u, h, s, b), gr.at[u, 13 + i])
                    if u not in LATE:
                        a = me_a[h] if s == 0 else ring(me_a[h], -OFFS[s - 1])
                        gsend(u, 29 + i, sub(u, h, a, b, d * 16), peer(h, db=off))
                    elif s // 2 == d:
                        gsend(u, 29 + i, g_part(u, h, s, b), peer(h, db=off))
        if u in LATE:
            g_swap(u, 1)

    def g_done(u):
        for s in range(4):
            for h in range(2):
                b = ring(me_b[h], 2)
                for d in range(2):
                    i = 29 + h * 8 + s * 2 + d
                    if u not in LATE:
                        a = me_a[h] if s == 0 else ring(me_a[h], -OFFS[s - 1])
                        arrived(sub(u, h, a, b, d * 16), gr.at[u, i])
                    elif s // 2 == d:
                        arrived(g_part(u, h, s, b), gr.at[u, i])
        if u in LATE:
            g_swap(u, 2)

    def g_swapped(u, h):
        for k in range(4):
            arrived(plane(u, h, ring(me_b[h], (0, 1, -1, 2)[k]), pair_row), gr.at[u, 45 + h * 4 + k])

    def rows_of(i, r):
        return X[i, pl.ds(2 * r, 2)].reshape(256, Q)

    def gate_up(q, first=False):
        def step(r, _):
            x = rows_of(q, r)
            rows = pl.ds(pl.multiple_of(r * 256, 256), 256)
            g = mm_nt(x, WG[q])
            u = mm_nt(x, WU[q])
            if first:
                gate[rows, :] = g
                up[rows, :] = u
            else:
                gate[rows, :] += g
                up[rows, :] += u
            return 0

        lax.fori_loop(0, 2, step, 0)

    def hidden():
        def step(r, _):
            rows = pl.ds(pl.multiple_of(r * 32, 32), 32)
            g = gate[rows, :]
            hid[rows, :] = (g * jax.nn.sigmoid(g) * up[rows, :]).astype(BF16)
            return 0

        lax.fori_loop(0, 16, step, 0)

    def factors():
        def step(r, _):
            rows = pl.ds(pl.multiple_of(r * 32, 32), 32)
            g = gate[rows, :]
            sig = jax.nn.sigmoid(g)
            gate[rows, :] = up[rows, :] * sig * (1.0 + g * (1.0 - sig))
            up[rows, :] = g * sig
            return 0

        lax.fori_loop(0, 16, step, 0)

    def backward(dst, factor):
        def step(r, _):
            rows = pl.ds(pl.multiple_of(r * 64, 64), 64)
            dst[rows, :] = (dhid[rows, :] * factor[rows, :]).astype(BF16)
            return 0

        lax.fori_loop(0, 8, step, 0)

    def transpose(src, dst):
        for r in range(4):
            dst[:, r * 128:(r + 1) * 128] = src[r * 128:(r + 1) * 128, :].astype(F32).T.astype(BF16)

    def output_part(q):
        def step(r, _):
            rows = pl.ds(pl.multiple_of(r * 256, 256), 256)
            PS[q, pl.ds(2 * r, 2)] = mm(hid[rows, :], WD[q]).astype(BF16).reshape(2, 4, 32, Q)
            return 0

        lax.fori_loop(0, 2, step, 0)

    def dhidden_part(u, first):
        for h in range(2):
            def step(r, _):
                rows = pl.ds(pl.multiple_of(r * 256, 256), 256)
                x = X[base[u] + h, pl.ds(2 * r, 2), :, :, cols[u]]
                v = mm_nt(x.reshape(256, x.shape[-1]), WD[base[u] - 4 + h, :, cols[u]])
                if first and h == 0:
                    dhid[rows, :] = v
                else:
                    dhid[rows, :] += v
                return 0

            lax.fori_loop(0, 2, step, 0)

    def input_part(q):
        def step(r, _):
            rows = pl.ds(pl.multiple_of(r * 256, 256), 256)
            v = mm(dgate[rows, :], WG[q]) + mm(dup[rows, :], WU[q])
            PS[4 + q, pl.ds(2 * r, 2)] = v.astype(BF16).reshape(2, 4, 32, Q)
            return 0

        lax.fori_loop(0, 2, step, 0)

    def chunk(v, h, b, row, n):
        tail = (pl.ds(row, n), slice(None))
        i = (v // 2) * 4 + (v % 2) * 2 + h
        return (i, b, slice(None)) + tail if h == 0 else (i, slice(None), b) + tail

    def s_first(v):
        for h in range(2):
            for d, off in enumerate((1, -1)):
                k = h * 6 + d * 3
                far, near = ring(me_b[h], 2), ring(me_b[h], off)
                send(PS.at[chunk(v, h, far, d * 16, 16)], RF.at[v, h, d], ss.at[v, k], sr.at[v, k], peer(h, db=off))
                o = (1 - d) * 16
                send(
                    PS.at[chunk(v, h, near, o, 16)], R1.at[v, h, d, :, pl.ds(o, 16)],
                    ss.at[v, k + 1], sr.at[v, k + 1], peer(h, db=off),
                )

    def s_join(v):
        for h in range(2):
            for d, off in enumerate((1, -1)):
                k = h * 6 + d * 3
                near, o = ring(me_b[h], off), d * 16
                arrived(RF.at[v, h, d], sr.at[v, k])
                RF[v, h, d] = (
                    RF[v, h, d].astype(F32) + PS[chunk(v, h, near, o, 16)].astype(F32)
                ).astype(BF16)
                send(
                    RF.at[v, h, d], R1.at[v, h, d, :, pl.ds(o, 16)],
                    ss.at[v, k + 2], sr.at[v, k + 2], peer(h, db=off),
                )

    def s_second(v):
        for h in range(2):
            for d in range(2):
                k = h * 6 + d * 3
                arrived(R1.at[v, h, d, :, pl.ds((1 - d) * 16, 16)], sr.at[v, k + 1])
                arrived(R1.at[v, h, d, :, pl.ds(d * 16, 16)], sr.at[v, k + 2])
            i = (v // 2) * 4 + (v % 2) * 2 + h

            def total(a):
                own = PS[(i,) + at(h, a, me_b[h])].astype(F32)
                return own + R1[v, h, 0, a].astype(F32) + R1[v, h, 1, a].astype(F32)

            for s, off in enumerate(OFFS):
                a = ring(me_a[h], off)
                mine = (i,) + at(h, a, me_b[h])
                PS[mine] = total(a).astype(BF16)
                k = 12 + h * 3 + s
                send(PS.at[mine], R2.at[v, h, s], ss.at[v, k], sr.at[v, k], peer(h, da=off))
            SO[v, h] = total(me_a[h])

    def s_third(v):
        for h in range(2):
            for s in range(3):
                arrived(R2.at[v, h, s], sr.at[v, 12 + h * 3 + s])
            SO[v, h] = (
                SO[v, h] + R2[v, h, 0].astype(F32) + R2[v, h, 1].astype(F32) + R2[v, h, 2].astype(F32)
            )
            TO[v, h] = SO[v, h, pl.ds(my_row, 16)]
            TS[v, h] = SO[v, h, pl.ds(pair_row, 16)].astype(BF16)
        send(TS.at[v], R3.at[v], ss.at[v, 18], sr.at[v, 18], h_pair)

    stores = []

    def s_finish(v):
        arrived(R3.at[v], sr.at[v, 18])
        for h in range(2):
            q = (v % 2) * 2 + h
            OB[v // 2, :, q * Q:(q + 1) * Q] = (TO[v, h] + R3[v, h].astype(F32)).astype(BF16)
        if v % 2 == 1:
            cp = pltpu.make_async_copy(OB.at[v // 2], (out, ig)[v // 2], ls.at[20 + v // 2])
            cp.start()
            stores.append(cp)

    lhs, x0 = (hidT, dgT, duT), (4, 0, 0)
    jobs = {}

    def w_part(j, n):
        arr, w = j % 3, (1 - xl) if j < 3 else xl
        part = PARTS[n]
        if j >= 2:
            old = jobs[j - 2, n]
            old.wait_send()
            started[:] = [cp for cp in started if cp is not old]

        for k in range(2):
            quarter = w * 2 + ((1 - c), c)[k]
            slot = (6 + j % 2, j)[k]
            xb = X[x0[arr] + quarter, :, :, :, part].reshape(T, part.size)
            WB[slot, :, part] = mm(lhs[arr][...], xb).astype(BF16)
            if k == 0:
                jobs[j, n] = send(
                    WB.at[slot, :, part], CR.at[j, :, part], cs.at[j, n], cr.at[j, n], core_pair
                )

    def w_cross(j, n):
        part = PARTS[n]
        arrived(CR.at[j, :, part], cr.at[j, n])

        def step(r, _):
            rows = pl.ds(pl.multiple_of(r * 64, 64), 64)
            WB[j, rows, part] = (WB[j, rows, part].astype(F32) + CR[j, rows, part].astype(F32)).astype(BF16)
            return 0

        lax.fori_loop(0, 7, step, 0)
        send(WB.at[j, :, part], XR.at[j, :, part], xs.at[j, n], xr.at[j, n], x_pair)

    def w_finish(arr, n):
        j = 3 + arr
        part = PARTS[n]
        arrived(CR.at[j, :, part], cr.at[j, n])
        arrived(XR.at[arr, :, part], xr.at[arr, n])

        def step(r, _):
            rows = pl.ds(pl.multiple_of(r * 64, 64), 64)
            v = WB[j, rows, part].astype(F32) + CR[j, rows, part].astype(F32) + XR[arr, rows, part].astype(F32)
            WB[j, rows, part] = v.astype(BF16)
            return 0

        lax.fori_loop(0, 7, step, 0)
        cp = pltpu.make_async_copy(WB.at[j, :, part], (dg, gg, ug)[arr].at[:, part], ls.at[22 + arr * 2 + n])
        cp.start()
        stores.append(cp)

    for cp in loads:
        cp.wait()
    g_pair(1)
    g_start(0)
    g_start(1)
    g_pair(2)
    g_pair(3)
    g_pair(4)
    g_own(1)
    g_mid(0)
    g_forward(0)
    g_relay(1)
    g_start(2)
    g_mid(1)
    g_own(2)
    g_done(0)
    for cp in wloads:
        cp.wait()
    g_forward(1)
    g_mid(2)
    g_start(3)
    g_done(1)
    g_own(3)
    gate_up(2, True)
    gate_up(3)
    g_forward(2)
    g_mid(3)
    g_start(4)
    g_swapped(0, 0)
    gate_up(0)
    g_own(4)
    g_swapped(0, 1)
    gate_up(1)
    hidden()
    transpose(hid, hidT)
    g_done(2)
    w_part(0, 0)
    g_forward(3)
    g_mid(4, (1, ))
    w_cross(0, 0)
    g_mid(4, (2, 3))
    g_done(3)
    w_part(0, 1)
    output_part(0)
    w_cross(0, 1)
    output_part(1)
    g_forward(4)
    factors()
    s_first(0)
    output_part(2)
    dhidden_part(2, True)
    dhidden_part(3, False)
    output_part(3)
    s_first(1)
    g_done(4)
    dhidden_part(4, False)
    backward(dgate, gate)
    transpose(dgate, dgT)
    w_part(1, 0)
    w_part(1, 1)
    backward(dup, up)
    w_cross(1, 0)
    w_cross(1, 1)
    s_join(0)
    input_part(0)
    input_part(1)
    s_first(2)
    transpose(dup, duT)
    w_part(2, 0)
    s_join(1)
    w_part(2, 1)
    w_cross(2, 0)
    s_second(0)
    input_part(2)
    input_part(3)
    s_first(3)
    s_second(1)
    s_join(2)
    s_third(0)
    w_part(3, 0)
    w_part(3, 1)
    s_join(3)
    s_third(1)
    w_cross(2, 1)
    w_part(4, 0)
    w_part(4, 1)
    s_second(2)
    w_part(5, 0)
    w_part(5, 1)
    w_finish(0, 0)
    w_finish(0, 1)
    s_third(2)
    s_second(3)
    s_finish(0)
    s_finish(1)
    w_finish(1, 0)
    s_third(3)
    w_finish(1, 1)
    s_finish(2)
    w_finish(2, 0)
    s_finish(3)
    w_finish(2, 1)
    for cp in started:
        cp.wait_send()
    for cp in stores:
        cp.wait()


def store(*refs):
    sems = refs[15]
    into = [pltpu.make_async_copy(refs[i], refs[10 + i], sems.at[i]) for i in range(5)]
    back = [pltpu.make_async_copy(refs[10 + i], refs[5 + i], sems.at[5 + i]) for i in range(5)]
    for cp in into:
        cp.start()
    for a, b in zip(into, back):
        a.wait()
        b.start()
    for cp in back:
        cp.wait()


def body(tokens, cotangent, gate_weight, up_weight, down_weight):
    any_spec = pl.BlockSpec(memory_space=pl.ANY)
    vm, dma = pltpu.VMEM, pltpu.SemaphoreType.DMA
    blocks = (4, 4, 32, Q)
    shapes = [jax.ShapeDtypeStruct((16, D), BF16)] * 2 + [jax.ShapeDtypeStruct((H, Q), BF16)] * 3
    results = pl.pallas_call(
        kernel,
        out_shape=shapes,
        in_specs=[any_spec] * 5,
        out_specs=[any_spec] * 5,
        scratch_shapes=[
            vm((8,) + blocks, BF16),
            vm((4, H, Q), BF16), vm((4, H, Q), BF16), vm((4, H, Q), BF16),
            vm((T, H), F32), vm((T, H), F32), vm((T, H), F32),
            vm((T, H), BF16), vm((T, H), BF16), vm((T, H), BF16),
            vm((H, T), BF16), vm((H, T), BF16), vm((H, T), BF16),
            vm((8,) + blocks, BF16),
            vm((4, 2, 2, 4, 32, Q), BF16),
            vm((4, 2, 2, 4, 16, Q), BF16),
            vm((4, 2, 3, 32, Q), BF16),
            vm((4, 2, 16, Q), BF16), vm((4, 2, 16, Q), BF16),
            vm((4, 2, 16, Q), F32), vm((4, 2, 32, Q), F32),
            vm((2, 16, D), BF16),
            vm((8, H, Q), BF16), vm((6, H, Q), BF16), vm((3, H, Q), BF16),
            dma((28,)), dma((5, 53)), dma((5, 53)), dma((4, 19)), dma((4, 19)),
            dma((6, 2)), dma((6, 2)), dma((3, 2)), dma((3, 2)),
        ],
        compiler_params=pltpu.CompilerParams(
            collective_id=0, has_side_effects=True, vmem_limit_bytes=62 * 1024 * 1024
        ),
        cost_estimate=pl.CostEstimate(flops=17_000_000_000, bytes_accessed=15_000_000, transcendentals=460_000),
    )(tokens, cotangent, gate_weight.T, up_weight.T, down_weight)
    output, input_grad, gate_grad, up_grad, down_grad = pl.pallas_call(
        store,
        out_shape=shapes,
        in_specs=[any_spec] * 5,
        out_specs=[any_spec] * 5,
        scratch_shapes=[vm(x.shape, BF16) for x in shapes] + [dma((10,))],
    )(*results)
    return output, input_grad, gate_grad.T, up_grad.T, down_grad


def solution(mesh):
    placed = (
        P(("dp", "tensor"), None),
        P(("dp", "tensor"), None),
        P(None, "tensor"),
        P(None, "tensor"),
        P("tensor", None),
    )
    return jax.shard_map(
        body,
        mesh=mesh,
        in_specs=placed,
        out_specs=(
            P(("dp", "tensor"), None),
            P(("dp", "tensor"), None),
            P("dp", "tensor"),
            P("dp", "tensor"),
            P("tensor", "dp"),
        ),
        check_vma=False,
    )
```

```python
import jax
import jax.numpy as jnp
from jax import lax
from jax.experimental import pallas as pl
from jax.experimental.pallas import tpu as pltpu
from jax.sharding import PartitionSpec as P

MESH = pl.DeviceIdType.MESH
BF16, F32 = jnp.bfloat16, jnp.float32
T, D, H, Q = 512, 4096, 448, 1024
PARTS = (pl.ds(0, 512), pl.ds(512, 512))


def mm(a, b):
    return jnp.dot(a, b, preferred_element_type=F32)


def mm_nt(a, b):
    return lax.dot_general(a, b, (((1,), (1,)), ((), ())), preferred_element_type=F32)


def kernel(
    tok, cot, wg, wu, wd,
    out, ig, gg, ug, dg,
    X, WG, WU, WD, gate, up, dhid, hid, dgate, dup, hidT, dgT, duT,
    PS, R1, RF, R2, R3, TS, TO, SO, OB, WB, CR, XR,
    ls, gs, gr, ss, sr, cs, cr, xs, xr,
):
    dp, t = lax.axis_index("dp"), lax.axis_index("tensor")
    xl, c = dp // 2, lax.rem(dp, 2)
    z, y, xh = t // 8, lax.rem(t // 2, 4), lax.rem(t, 2)

    def ring(v, off):
        return lax.rem(v + (off + 4) % 4, 4)

    def dev(zz, yy, hh=None):
        return (dp, zz * 8 + yy * 2 + (xh if hh is None else hh))

    x_pair = ((1 - xl) * 2 + c, t)
    core_pair = (xl * 2 + 1 - c, t)
    h_pair = dev(z, y, 1 - xh)
    my_row = pl.multiple_of(xh * 16, 16)
    pair_row = pl.multiple_of((1 - xh) * 16, 16)
    OFFS = (1, -1, 2)

    def at(h, a, b):
        return (b, a) if h == 0 else (a, b)

    me_a, me_b = (y, z), (z, y)

    def peer(h, da=0, db=0):
        return dev(*at(h, ring(me_a[h], da), ring(me_b[h], db)))

    started, gathers = [], []

    def send(src, dst, s, r, to):
        cp = pltpu.make_async_remote_copy(
            src_ref=src, dst_ref=dst, send_sem=s, recv_sem=r, device_id=to, device_id_type=MESH
        )
        cp.start()
        started.append(cp)
        return cp

    def arrived(ref, r):
        pltpu.make_async_copy(ref, ref, r).wait()

    barrier = pltpu.get_barrier_semaphore()
    peers = [x_pair, core_pair, h_pair]
    for off in OFFS:
        peers += [dev(ring(z, off), y), dev(z, ring(y, off))]
    for p in peers:
        pl.semaphore_signal(barrier, inc=1, device_id=p, device_id_type=MESH)

    loads = []
    for arr, ref in enumerate((tok, cot)):
        for q in range(4):
            cp = pltpu.make_async_copy(
                ref.at[:, pl.ds(q * Q, Q)], X.at[arr * 4 + q, z, y, pl.ds(my_row, 16)], ls.at[arr * 4 + q]
            )
            cp.start()
            loads.append(cp)
    wloads = []
    for i, (ref, dst) in enumerate(((wg, WG), (wu, WU), (wd, WD))):
        for q in range(4):
            wloads.append(pltpu.make_async_copy(ref.at[:, pl.ds(q * Q, Q)], dst.at[q], ls.at[8 + i * 4 + q]))
    for cp in wloads:
        cp.start()

    pl.semaphore_wait(barrier, len(peers))

    base = (0, 2, 4 + (1 - xl) * 2, 4 + (1 - xl) * 2, 4 + xl * 2)
    cols = (pl.ds(0, Q), pl.ds(0, Q), *PARTS, pl.ds(0, Q))

    def blk(u, h, a, b):
        return X.at[(base[u] + h,) + at(h, a, b) + (slice(None), cols[u])]

    def sub(u, h, a, b, row):
        return X.at[(base[u] + h,) + at(h, a, b) + (pl.ds(row, 16), cols[u])]

    def gsend(u, i, ref, to):
        gathers.append(send(ref, ref, gs.at[u, i], gr.at[u, i], to))
        started.pop()

    LATE = (0,)
    RELAY = (1,)

    def g_pair(u):
        gsend(u, 0, X.at[pl.ds(base[u], 2), z, y, pl.ds(my_row, 16), cols[u]], h_pair)

    def g_start(u):
        for s, off in enumerate(OFFS[:2] if u in RELAY else OFFS):
            for h in range(2):
                gsend(u, 1 + h * 6 + s, sub(u, h, me_a[h], me_b[h], my_row), peer(h, da=off))
        g_near(u, my_row, 13, 8)

    def g_near(u, row, i, step):
        for h in range(2):
            for d, off in enumerate((1, -1)):
                gsend(u, i + h * step + d, sub(u, h, me_a[h], me_b[h], row), peer(h, db=off))

    def g_own(u):
        arrived(X.at[pl.ds(base[u], 2), z, y, pl.ds(pair_row, 16), cols[u]], gr.at[u, 0])
        for s, off in enumerate(OFFS[:2] if u in RELAY else OFFS):
            for h in range(2):
                gsend(u, 4 + h * 6 + s, sub(u, h, me_a[h], me_b[h], pair_row), peer(h, da=off))
        g_near(u, pair_row, 45, 2)

    def g_relay(u):
        for h in range(2):
            low, high = ring(me_a[h], -1), ring(me_a[h], 1)
            ref = sub(u, h, low, me_b[h], my_row)
            arrived(ref, gr.at[u, 1 + h * 6])
            gsend(u, 3 + h * 6, ref, peer(h, da=1))
            ref = sub(u, h, high, me_b[h], pair_row)
            arrived(ref, gr.at[u, 5 + h * 6])
            gsend(u, 6 + h * 6, ref, peer(h, da=-1))

    def g_part(u, h, s, b):
        a = me_a[h] if s == 0 else ring(me_a[h], -OFFS[s - 1])
        return sub(u, h, a, b, my_row) if u in LATE else blk(u, h, a, b)

    def g_mid(u, sides=(1, 2, 3)):
        for s in sides:
            for h in range(2):
                a = ring(me_a[h], -OFFS[s - 1])
                mine = sub(u, h, a, me_b[h], my_row)
                if u not in RELAY or s != 1:
                    arrived(mine, gr.at[u, s + h * 6])
                if u not in LATE and (u not in RELAY or s != 2):
                    arrived(sub(u, h, a, me_b[h], pair_row), gr.at[u, 3 + s + h * 6])
                for d, off in enumerate((1, -1)):
                    gsend(u, 13 + h * 8 + s * 2 + d, g_part(u, h, s, me_b[h]), peer(h, db=off))
        if u in LATE:
            g_swap(u, 0)

    def plane(u, h, b, row):
        tail = (pl.ds(row, 16), cols[u])
        i = base[u] + h
        return X.at[(i, b, slice(None)) + tail] if h == 0 else X.at[(i, slice(None), b) + tail]

    def g_swap(u, stage):
        for h in range(2):
            for k in ((0,), (1, 2), (3,))[stage]:
                gsend(u, 45 + h * 4 + k, plane(u, h, ring(me_b[h], (0, 1, -1, 2)[k]), my_row), h_pair)

    def g_forward(u):
        for s in range(4):
            for h in range(2):
                for d, off in enumerate((1, -1)):
                    b = ring(me_b[h], -off)
                    i = h * 8 + s * 2 + d
                    if s == 0 and u not in LATE:
                        arrived(sub(u, h, me_a[h], b, my_row), gr.at[u, 13 + i])
                        arrived(sub(u, h, me_a[h], b, pair_row), gr.at[u, 45 + h * 2 + d])
                    else:
                        arrived(g_part(u, h, s, b), gr.at[u, 13 + i])
                    if u not in LATE:
                        a = me_a[h] if s == 0 else ring(me_a[h], -OFFS[s - 1])
                        gsend(u, 29 + i, sub(u, h, a, b, d * 16), peer(h, db=off))
                    elif s // 2 == d:
                        gsend(u, 29 + i, g_part(u, h, s, b), peer(h, db=off))
        if u in LATE:
            g_swap(u, 1)

    def g_done(u):
        for s in range(4):
            for h in range(2):
                b = ring(me_b[h], 2)
                for d in range(2):
                    i = 29 + h * 8 + s * 2 + d
                    if u not in LATE:
                        a = me_a[h] if s == 0 else ring(me_a[h], -OFFS[s - 1])
                        arrived(sub(u, h, a, b, d * 16), gr.at[u, i])
                    elif s // 2 == d:
                        arrived(g_part(u, h, s, b), gr.at[u, i])
        if u in LATE:
            g_swap(u, 2)

    def g_swapped(u, h):
        for k in range(4):
            arrived(plane(u, h, ring(me_b[h], (0, 1, -1, 2)[k]), pair_row), gr.at[u, 45 + h * 4 + k])

    def rows_of(i, r):
        return X[i, pl.ds(2 * r, 2)].reshape(256, Q)

    def gate_up(q, first=False):
        def step(r, _):
            x = rows_of(q, r)
            rows = pl.ds(pl.multiple_of(r * 256, 256), 256)
            g = mm_nt(x, WG[q])
            u = mm_nt(x, WU[q])
            if first:
                gate[rows, :] = g
                up[rows, :] = u
            else:
                gate[rows, :] += g
                up[rows, :] += u
            return 0

        lax.fori_loop(0, 2, step, 0)

    def hidden():
        def step(r, _):
            rows = pl.ds(pl.multiple_of(r * 32, 32), 32)
            g = gate[rows, :]
            hid[rows, :] = (g * jax.nn.sigmoid(g) * up[rows, :]).astype(BF16)
            return 0

        lax.fori_loop(0, 16, step, 0)

    def factors():
        def step(r, _):
            rows = pl.ds(pl.multiple_of(r * 32, 32), 32)
            g = gate[rows, :]
            sig = jax.nn.sigmoid(g)
            gate[rows, :] = up[rows, :] * sig * (1.0 + g * (1.0 - sig))
            up[rows, :] = g * sig
            return 0

        lax.fori_loop(0, 16, step, 0)

    def backward(dst, factor):
        def step(r, _):
            rows = pl.ds(pl.multiple_of(r * 64, 64), 64)
            dst[rows, :] = (dhid[rows, :] * factor[rows, :]).astype(BF16)
            return 0

        lax.fori_loop(0, 8, step, 0)

    def transpose(src, dst):
        for r in range(4):
            dst[:, r * 128:(r + 1) * 128] = src[r * 128:(r + 1) * 128, :].astype(F32).T.astype(BF16)

    def output_part(q):
        def step(r, _):
            rows = pl.ds(pl.multiple_of(r * 256, 256), 256)
            PS[q, pl.ds(2 * r, 2)] = mm(hid[rows, :], WD[q]).astype(BF16).reshape(2, 4, 32, Q)
            return 0

        lax.fori_loop(0, 2, step, 0)

    def dhidden_part(u, first):
        for h in range(2):
            def step(r, _):
                rows = pl.ds(pl.multiple_of(r * 256, 256), 256)
                x = X[base[u] + h, pl.ds(2 * r, 2), :, :, cols[u]]
                v = mm_nt(x.reshape(256, x.shape[-1]), WD[base[u] - 4 + h, :, cols[u]])
                if first and h == 0:
                    dhid[rows, :] = v
                else:
                    dhid[rows, :] += v
                return 0

            lax.fori_loop(0, 2, step, 0)

    def input_part(q):
        def step(r, _):
            rows = pl.ds(pl.multiple_of(r * 256, 256), 256)
            v = mm(dgate[rows, :], WG[q]) + mm(dup[rows, :], WU[q])
            PS[4 + q, pl.ds(2 * r, 2)] = v.astype(BF16).reshape(2, 4, 32, Q)
            return 0

        lax.fori_loop(0, 2, step, 0)

    def chunk(v, h, b, row, n):
        tail = (pl.ds(row, n), slice(None))
        i = (v // 2) * 4 + (v % 2) * 2 + h
        return (i, b, slice(None)) + tail if h == 0 else (i, slice(None), b) + tail

    def s_first(v):
        for h in range(2):
            for d, off in enumerate((1, -1)):
                k = h * 6 + d * 3
                far, near = ring(me_b[h], 2), ring(me_b[h], off)
                send(PS.at[chunk(v, h, far, d * 16, 16)], RF.at[v, h, d], ss.at[v, k], sr.at[v, k], peer(h, db=off))
                o = (1 - d) * 16
                send(
                    PS.at[chunk(v, h, near, o, 16)], R1.at[v, h, d, :, pl.ds(o, 16)],
                    ss.at[v, k + 1], sr.at[v, k + 1], peer(h, db=off),
                )

    def s_join(v):
        for h in range(2):
            for d, off in enumerate((1, -1)):
                k = h * 6 + d * 3
                near, o = ring(me_b[h], off), d * 16
                arrived(RF.at[v, h, d], sr.at[v, k])
                RF[v, h, d] = (
                    RF[v, h, d].astype(F32) + PS[chunk(v, h, near, o, 16)].astype(F32)
                ).astype(BF16)
                send(
                    RF.at[v, h, d], R1.at[v, h, d, :, pl.ds(o, 16)],
                    ss.at[v, k + 2], sr.at[v, k + 2], peer(h, db=off),
                )

    def s_second(v):
        for h in range(2):
            for d in range(2):
                k = h * 6 + d * 3
                arrived(R1.at[v, h, d, :, pl.ds((1 - d) * 16, 16)], sr.at[v, k + 1])
                arrived(R1.at[v, h, d, :, pl.ds(d * 16, 16)], sr.at[v, k + 2])
            i = (v // 2) * 4 + (v % 2) * 2 + h

            def total(a):
                own = PS[(i,) + at(h, a, me_b[h])].astype(F32)
                return own + R1[v, h, 0, a].astype(F32) + R1[v, h, 1, a].astype(F32)

            for s, off in enumerate(OFFS):
                a = ring(me_a[h], off)
                mine = (i,) + at(h, a, me_b[h])
                PS[mine] = total(a).astype(BF16)
                k = 12 + h * 3 + s
                send(PS.at[mine], R2.at[v, h, s], ss.at[v, k], sr.at[v, k], peer(h, da=off))
            SO[v, h] = total(me_a[h])

    def s_third(v):
        for h in range(2):
            for s in range(3):
                arrived(R2.at[v, h, s], sr.at[v, 12 + h * 3 + s])
            SO[v, h] = (
                SO[v, h] + R2[v, h, 0].astype(F32) + R2[v, h, 1].astype(F32) + R2[v, h, 2].astype(F32)
            )
            TO[v, h] = SO[v, h, pl.ds(my_row, 16)]
            TS[v, h] = SO[v, h, pl.ds(pair_row, 16)].astype(BF16)
        send(TS.at[v], R3.at[v], ss.at[v, 18], sr.at[v, 18], h_pair)

    stores = []

    def s_finish(v):
        arrived(R3.at[v], sr.at[v, 18])
        for h in range(2):
            q = (v % 2) * 2 + h
            OB[v // 2, :, q * Q:(q + 1) * Q] = (TO[v, h] + R3[v, h].astype(F32)).astype(BF16)
        if v % 2 == 1:
            cp = pltpu.make_async_copy(OB.at[v // 2], (out, ig)[v // 2], ls.at[20 + v // 2])
            cp.start()
            stores.append(cp)

    lhs, x0 = (hidT, dgT, duT), (4, 0, 0)
    jobs = {}

    def w_part(j, n):
        arr, w = j % 3, (1 - xl) if j < 3 else xl
        part = PARTS[n]
        if j >= 2:
            old = jobs[j - 2, n]
            old.wait_send()
            started[:] = [cp for cp in started if cp is not old]

        for k in range(2):
            quarter = w * 2 + ((1 - c), c)[k]
            slot = (6 + j % 2, j)[k]
            xb = X[x0[arr] + quarter, :, :, :, part].reshape(T, part.size)
            WB[slot, :, part] = mm(lhs[arr][...], xb).astype(BF16)
            if k == 0:
                jobs[j, n] = send(
                    WB.at[slot, :, part], CR.at[j, :, part], cs.at[j, n], cr.at[j, n], core_pair
                )

    def w_cross(j, n):
        part = PARTS[n]
        arrived(CR.at[j, :, part], cr.at[j, n])

        def step(r, _):
            rows = pl.ds(pl.multiple_of(r * 64, 64), 64)
            WB[j, rows, part] = (WB[j, rows, part].astype(F32) + CR[j, rows, part].astype(F32)).astype(BF16)
            return 0

        lax.fori_loop(0, 7, step, 0)
        send(WB.at[j, :, part], XR.at[j, :, part], xs.at[j, n], xr.at[j, n], x_pair)

    def w_finish(arr, n):
        j = 3 + arr
        part = PARTS[n]
        arrived(CR.at[j, :, part], cr.at[j, n])
        arrived(XR.at[arr, :, part], xr.at[arr, n])

        def step(r, _):
            rows = pl.ds(pl.multiple_of(r * 64, 64), 64)
            v = WB[j, rows, part].astype(F32) + CR[j, rows, part].astype(F32) + XR[arr, rows, part].astype(F32)
            WB[j, rows, part] = v.astype(BF16)
            return 0

        lax.fori_loop(0, 7, step, 0)
        cp = pltpu.make_async_copy(WB.at[j, :, part], (dg, gg, ug)[arr].at[:, part], ls.at[22 + arr * 2 + n])
        cp.start()
        stores.append(cp)

    for cp in loads:
        cp.wait()
    g_pair(1)
    g_start(0)
    g_start(1)
    g_pair(2)
    g_pair(3)
    g_pair(4)
    g_own(1)
    g_mid(0)
    g_forward(0)
    g_relay(1)
    g_start(2)
    g_mid(1)
    g_own(2)
    g_done(0)
    for cp in wloads:
        cp.wait()
    g_forward(1)
    g_mid(2)
    g_start(3)
    g_done(1)
    g_own(3)
    gate_up(2, True)
    gate_up(3)
    g_forward(2)
    g_mid(3)
    g_start(4)
    g_swapped(0, 0)
    gate_up(0)
    g_own(4)
    g_swapped(0, 1)
    gate_up(1)
    hidden()
    transpose(hid, hidT)
    g_done(2)
    w_part(0, 0)
    g_forward(3)
    g_mid(4, (1, ))
    w_cross(0, 0)
    g_mid(4, (2, 3))
    g_done(3)
    w_part(0, 1)
    output_part(0)
    w_cross(0, 1)
    output_part(1)
    g_forward(4)
    factors()
    s_first(0)
    output_part(2)
    dhidden_part(2, True)
    dhidden_part(3, False)
    output_part(3)
    s_first(1)
    g_done(4)
    dhidden_part(4, False)
    backward(dgate, gate)
    transpose(dgate, dgT)
    w_part(1, 0)
    w_part(1, 1)
    backward(dup, up)
    w_cross(1, 0)
    w_cross(1, 1)
    s_join(0)
    input_part(0)
    input_part(1)
    s_first(2)
    transpose(dup, duT)
    w_part(2, 0)
    s_join(1)
    w_part(2, 1)
    w_cross(2, 0)
    s_second(0)
    input_part(2)
    input_part(3)
    s_first(3)
    s_second(1)
    s_join(2)
    s_third(0)
    w_part(3, 0)
    w_part(3, 1)
    s_join(3)
    s_third(1)
    w_cross(2, 1)
    w_part(4, 0)
    w_part(4, 1)
    s_second(2)
    w_part(5, 0)
    w_part(5, 1)
    for cp in gathers:
        cp.wait_send()
    w_finish(0, 0)
    w_finish(0, 1)
    s_third(2)
    s_second(3)
    s_finish(0)
    s_finish(1)
    w_finish(1, 0)
    s_third(3)
    w_finish(1, 1)
    s_finish(2)
    w_finish(2, 0)
    s_finish(3)
    w_finish(2, 1)
    for cp in started:
        cp.wait_send()
    for cp in stores:
        cp.wait()


def store(*refs):
    sems = refs[15]
    into = [pltpu.make_async_copy(refs[i], refs[10 + i], sems.at[i]) for i in range(5)]
    back = [pltpu.make_async_copy(refs[10 + i], refs[5 + i], sems.at[5 + i]) for i in range(5)]
    for cp in into:
        cp.start()
    for a, b in zip(into, back):
        a.wait()
        b.start()
    for cp in back:
        cp.wait()


def body(tokens, cotangent, gate_weight, up_weight, down_weight):
    any_spec = pl.BlockSpec(memory_space=pl.ANY)
    vm, dma = pltpu.VMEM, pltpu.SemaphoreType.DMA
    blocks = (4, 4, 32, Q)
    shapes = [jax.ShapeDtypeStruct((16, D), BF16)] * 2 + [jax.ShapeDtypeStruct((H, Q), BF16)] * 3
    results = pl.pallas_call(
        kernel,
        out_shape=shapes,
        in_specs=[any_spec] * 5,
        out_specs=[any_spec] * 5,
        scratch_shapes=[
            vm((8,) + blocks, BF16),
            vm((4, H, Q), BF16), vm((4, H, Q), BF16), vm((4, H, Q), BF16),
            vm((T, H), F32), vm((T, H), F32), vm((T, H), F32),
            vm((T, H), BF16), vm((T, H), BF16), vm((T, H), BF16),
            vm((H, T), BF16), vm((H, T), BF16), vm((H, T), BF16),
            vm((8,) + blocks, BF16),
            vm((4, 2, 2, 4, 32, Q), BF16),
            vm((4, 2, 2, 4, 16, Q), BF16),
            vm((4, 2, 3, 32, Q), BF16),
            vm((4, 2, 16, Q), BF16), vm((4, 2, 16, Q), BF16),
            vm((4, 2, 16, Q), F32), vm((4, 2, 32, Q), F32),
            vm((2, 16, D), BF16),
            vm((8, H, Q), BF16), vm((6, H, Q), BF16), vm((3, H, Q), BF16),
            dma((28,)), dma((5, 53)), dma((5, 53)), dma((4, 19)), dma((4, 19)),
            dma((6, 2)), dma((6, 2)), dma((3, 2)), dma((3, 2)),
        ],
        compiler_params=pltpu.CompilerParams(
            collective_id=0, has_side_effects=True, vmem_limit_bytes=62 * 1024 * 1024
        ),
        cost_estimate=pl.CostEstimate(flops=17_000_000_000, bytes_accessed=15_000_000, transcendentals=460_000),
    )(tokens, cotangent, gate_weight.T, up_weight.T, down_weight)
    output, input_grad, gate_grad, up_grad, down_grad = pl.pallas_call(
        store,
        out_shape=shapes,
        in_specs=[any_spec] * 5,
        out_specs=[any_spec] * 5,
        scratch_shapes=[vm(x.shape, BF16) for x in shapes] + [dma((10,))],
    )(*results)
    return output, input_grad, gate_grad.T, up_grad.T, down_grad


def solution(mesh):
    placed = (
        P(("dp", "tensor"), None),
        P(("dp", "tensor"), None),
        P(None, "tensor"),
        P(None, "tensor"),
        P("tensor", None),
    )
    return jax.shard_map(
        body,
        mesh=mesh,
        in_specs=placed,
        out_specs=(
            P(("dp", "tensor"), None),
            P(("dp", "tensor"), None),
            P("dp", "tensor"),
            P("dp", "tensor"),
            P("tensor", "dp"),
        ),
        check_vma=False,
    )
```
